128 devices in a mesh: dp: 16 (over x, z), cent: 8 (over y, core).
Axes of the slice: x: 4, y: 4, z: 4, core: 2. Of those that a mesh axis runs over, the one named last changes fastest.
Arguments:
- embeddings: bfloat16 [16384, 4096], P('dp'), may hold values from -15 to 15
- centroids: bfloat16 [8192, 4096], P('cent', 'dp'), may hold values from -12 to 12
Outputs:
- shares: bfloat16 [16384, 8192], P('dp', 'cent')
- new_centroids: bfloat16 [8192, 4096], P('cent', 'dp')
The draws below stay inside these ranges and needn't reach their ends.
All inputs are finite; a program needn't handle non-finite values.
Results may differ from the reference program's by a relative error of at most 0.0034.
Values may be sent and summed in bfloat16 or wider, within the bound.
No kernel may reach another device: no remote copies, remote signals or barrier semaphores. Data moves between devices by JAX's collectives and lax.ppermute only.
A program may use at most 128 MiB of HBM per device.

```python
import jax
import jax.numpy as jnp
from jax import lax

D = 4096
K = 8192
ROUNDS = 3
TOKENS = 16384


def group_count():
    return max(4, min(64, K // 128))


def shared_means(key):
    return jnp.clip(jax.random.normal(key, (group_count(), D), jnp.float32), -5.0, 5.0)


def draw_embeddings(key, part):
    means = shared_means(key)
    key = jax.random.fold_in(key, 11)
    key_group, key_strength, key_noise = jax.random.split(key, 3)
    group_ids = jax.random.randint(key_group, (TOKENS,), 0, group_count())
    strength = jax.random.uniform(key_strength, (TOKENS, 1), jnp.float32, 0.5, 1.5)
    centre = strength * means[group_ids]
    noise = jnp.clip(jax.random.normal(key_noise, (TOKENS, D), jnp.float32), -6.0, 6.0)
    values = centre + noise
    return values.astype(jnp.bfloat16)


def draw_centroids(key, part):
    means = shared_means(key)
    key = jax.random.fold_in(key, 23)
    key_pick, key_count, key_mix, key_noise = jax.random.split(key, 4)
    picks = jax.random.randint(key_pick, (K, 4), 0, group_count())
    count = jax.random.randint(key_count, (K, 1), 2, 5)
    used = (jnp.arange(4)[None, :] < count).astype(jnp.float32)
    mixing = jax.random.uniform(key_mix, (K, 4), jnp.float32, 0.2, 1.0) * used
    mixing = mixing / jnp.sum(mixing, 1, keepdims=True)
    centre = jnp.zeros((K, D), jnp.float32)
    for slot in range(4):
        centre = centre + mixing[:, slot:slot + 1] * means[picks[:, slot]]
    noise = 0.7 * jnp.clip(jax.random.normal(key_noise, (K, D), jnp.float32), -6.0, 6.0)
    return (centre + noise).astype(jnp.bfloat16)


def setup_inputs(seed: int = 0) -> dict:
    seeds = jax.random.split(jax.random.key(seed), 3)
    embeddings = draw_embeddings(jax.random.fold_in(seeds[2], 71), 0)
    centroids = draw_centroids(jax.random.fold_in(seeds[2], 71), 0)
    return {"embeddings": embeddings, "centroids": centroids}


def reference(embeddings, centroids):
    rows_float = embeddings.astype(jnp.float32)
    normed = (rows_float * lax.rsqrt(lax.optimization_barrier(jnp.sum(rows_float * rows_float, 1, keepdims=True)) + 1e-06)).astype(jnp.bfloat16)
    cent_float = centroids.astype(jnp.float32)
    scale = lax.rsqrt(lax.optimization_barrier(jnp.sum(cent_float * cent_float, 1)) + 1e-06)
    scores = jnp.dot(normed, centroids.T, preferred_element_type=jnp.float32) * scale[None, :]
    weights = jnp.exp(scores * 20.0)
    target = TOKENS / K
    for sweep in range(ROUNDS):
        weights = weights * (target / lax.optimization_barrier(jnp.sum(weights, 0)))[None, :]
        weights = weights / lax.optimization_barrier(jnp.sum(weights, 1, keepdims=True))
    shares = weights.astype(jnp.bfloat16)
    col_mass = lax.optimization_barrier(jnp.sum(shares.astype(jnp.float32), 0))
    sums = jnp.dot(shares.T, embeddings, preferred_element_type=jnp.float32)
    new_centroids = (sums / col_mass[:, None]).astype(jnp.bfloat16)
    return (shares, new_centroids)
```

```python
import jax
import jax.numpy as jnp
from jax import lax
from jax.sharding import PartitionSpec as P

ROUNDS = 3
SIDE = 4
PACK = 0.25


def _x(step):
    return [
        (x * SIDE + z, ((x + step) % SIDE) * SIDE + z) for x in range(SIDE) for z in range(SIDE)
    ]


def _z(step):
    return [
        (x * SIDE + z, x * SIDE + (z + step) % SIDE) for x in range(SIDE) for z in range(SIDE)
    ]


def _send(value, axis, step):
    return lax.ppermute(value, "dp", axis(step))


def _ring_gather(block, axis):
    before = _send(block, axis, 1)
    after = _send(block, axis, -1)
    half = block.shape[0] // 2
    far_low = _send(before[:half], axis, 1)
    far_high = _send(after[half:], axis, -1)
    return block, after, (far_low, far_high), before


def _dot_rows(rows, block):
    return lax.dot_general(
        rows, block, (((1,), (1,)), ((), ())), preferred_element_type=jnp.float32
    )


def _all_sum(value, axis):
    members = lax.axis_size(axis)
    copies = jnp.broadcast_to(value[None], (members,) + value.shape)
    return jnp.sum(lax.all_to_all(copies, axis, 0, 0), 0)


def _squares(block):
    wide = block.astype(jnp.float32)
    return jnp.sum(wide * wide, 1)


def _gather_scores(first, second, block, rows):
    own, after, far, before = _ring_gather(block, first)
    panel = jnp.concatenate([own, after, jnp.concatenate(far, 0), before], 1)
    own, after, far, before = _ring_gather(panel, second)
    total = _dot_rows(rows[0], own)
    squares = _squares(own)
    total = total + _dot_rows(rows[1], after) + _dot_rows(rows[3], before)
    squares = squares + _squares(after) + _squares(before)
    far = jnp.concatenate(far, 0)
    return total + _dot_rows(rows[2], far), squares + _squares(far)


def _pack(value):
    return (value * PACK).astype(jnp.float16)


def _unpack(value):
    return value.astype(jnp.float32)


def _ring_scatter(part, axis, split):
    far_low, far_high = split(_pack(part(2)))
    low = _send(far_low, axis, 1)
    high = _send(far_high, axis, -1)
    after_low, after_high = split(part(1) * PACK)
    before_low, before_high = split(part(3) * PACK)
    after = jnp.concatenate([after_low + _unpack(low), after_high], 0).astype(jnp.float16)
    before = jnp.concatenate([before_low, before_high + _unpack(high)], 0).astype(jnp.float16)
    from_before = _send(after, axis, 1)
    from_after = _send(before, axis, -1)
    return part(0) * PACK + _unpack(from_before) + _unpack(from_after)


def _halves(value):
    half = value.shape[0] // 2
    return value[:half], value[half:]


def _scatter_sums(first, second, shares, rows):
    def part(offset):
        return lax.dot_general(
            shares, rows[offset], (((0,), (0,)), ((), ())), preferred_element_type=jnp.float32
        )

    line = _ring_scatter(part, first, _halves)
    width = line.shape[1] // SIDE

    def block(offset):
        return line[:, offset * width : (offset + 1) * width] / PACK

    return _ring_scatter(block, second, _halves) / PACK


def _relative(array, x, z):
    rows, features = array.shape
    grid = array.reshape(rows, SIDE, SIDE, features // (SIDE * SIDE))
    grid = jnp.roll(grid, (-x, -z), (1, 2))
    by_x = [grid[:, i].reshape(rows, -1) for i in range(SIDE)]
    by_z = [grid[:, :, i].reshape(rows, -1) for i in range(SIDE)]
    return by_x, by_z


def on_device(embeddings, centroids):
    row_count = embeddings.shape[0]
    local_k = centroids.shape[0]
    half = local_k // 2
    me = lax.axis_index("dp")
    x, z = me // SIDE, me % SIDE
    rows_float = embeddings.astype(jnp.float32)
    normed = (
        rows_float * lax.rsqrt(jnp.sum(rows_float * rows_float, 1, keepdims=True) + 1e-06)
    ).astype(jnp.bfloat16)
    normed_x, normed_z = _relative(normed, x, z)
    rows_x, rows_z = _relative(embeddings, x, z)
    score_a, square_a = _gather_scores(_z, _x, centroids[:half], normed_x)
    score_b, square_b = _gather_scores(_x, _z, centroids[half:], normed_z)
    scores = jnp.concatenate([score_a, score_b], 1)
    scale = lax.rsqrt(jnp.concatenate([square_a, square_b]) + 1e-06)
    weights = jnp.exp(scores * scale[None, :] * 20.0)
    target = row_count * lax.axis_size("dp") / (local_k * lax.axis_size("cent"))
    column = _all_sum(jnp.sum(weights, 0), "dp")
    for sweep in range(ROUNDS):
        column_scale = target / column
        row_sum = _all_sum(jnp.sum(weights * column_scale[None, :], 1), "cent")
        row_scale = 1.0 / row_sum
        if sweep + 1 < ROUNDS:
            column = _all_sum(jnp.sum(weights * row_scale[:, None], 0), "dp")
    shares = (weights * column_scale[None, :] * row_scale[:, None]).astype(jnp.bfloat16)
    mass = _all_sum(jnp.sum(shares.astype(jnp.float32), 0), "dp")
    sums_a = _scatter_sums(_x, _z, shares[:, :half], rows_x)
    sums_b = _scatter_sums(_z, _x, shares[:, half:], rows_z)
    sums = jnp.concatenate([sums_a, sums_b], 0)
    new_centroids = (sums / mass[:, None]).astype(jnp.bfloat16)
    return (shares, new_centroids)


def solution(mesh):
    in_specs = (P("dp", None), P("cent", "dp"))
    out_specs = (P("dp", "cent"), P("cent", "dp"))
    return jax.shard_map(
        on_device, mesh=mesh, in_specs=in_specs, out_specs=out_specs, check_vma=False
    )
```

```python
import jax
import jax.numpy as jnp
from jax import lax
from jax.experimental import pallas as pl
from jax.experimental.pallas import tpu as pltpu
from jax.sharding import PartitionSpec as P

ROUNDS = 3
SIDE = 4
PACK = 0.25


def _x(step):
    return [
        (x * SIDE + z, ((x + step) % SIDE) * SIDE + z) for x in range(SIDE) for z in range(SIDE)
    ]


def _z(step):
    return [
        (x * SIDE + z, x * SIDE + (z + step) % SIDE) for x in range(SIDE) for z in range(SIDE)
    ]


def _send(value, axis, step):
    return lax.ppermute(value, "dp", axis(step))


def _ring_gather(block, axis):
    before = _send(block, axis, 1)
    after = _send(block, axis, -1)
    half = block.shape[0] // 2
    far_low = _send(before[:half], axis, 1)
    far_high = _send(after[half:], axis, -1)
    return block, after, (far_low, far_high), before


def _dot_rows(rows, block):
    return lax.dot_general(
        rows, block, (((1,), (1,)), ((), ())), preferred_element_type=jnp.float32
    )


def _all_sum(value, axis):
    members = lax.axis_size(axis)
    copies = jnp.broadcast_to(value[None], (members,) + value.shape)
    return jnp.sum(lax.all_to_all(copies, axis, 0, 0), 0)


def _squares(block):
    wide = block.astype(jnp.float32)
    return jnp.sum(wide * wide, 1)


def _ring_panel(axis, block):
    own, after, far, before = _ring_gather(block, axis)
    return jnp.concatenate([own, after, jnp.concatenate(far, 0), before], 1)


def _gather_scores(axis, panel, rows):
    own, after, far, before = _ring_gather(panel, axis)
    total = _dot_rows(rows[0], own)
    squares = _squares(own)
    total = total + _dot_rows(rows[1], after) + _dot_rows(rows[3], before)
    squares = squares + _squares(after) + _squares(before)
    far = jnp.concatenate(far, 0)
    return total + _dot_rows(rows[2], far), squares + _squares(far)


def _pack(value):
    return value.astype(jnp.float16)


def _unpack(value):
    return value.astype(jnp.float32)


def _ring_scatter(part, axis, split):
    far_low, far_high = split(_pack(part(2)))
    low = _send(far_low, axis, 1)
    high = _send(far_high, axis, -1)
    after_low, after_high = split(part(1))
    before_low, before_high = split(part(3))
    after = jnp.concatenate([_pack(after_low + _unpack(low)), _pack(after_high)], 0)
    before = jnp.concatenate([_pack(before_low), _pack(before_high + _unpack(high))], 0)
    from_before = _send(after, axis, 1)
    from_after = _send(before, axis, -1)
    return part(0) + _unpack(from_before) + _unpack(from_after)


def _halves(value):
    half = value.shape[0] // 2
    return value[:half], value[half:]


def _scatter_sums(first, second, shares, rows):
    def part(offset):
        return lax.dot_general(
            shares, rows[offset], (((0,), (0,)), ((), ())), preferred_element_type=jnp.float32
        )

    line = _ring_scatter(part, first, _halves)
    width = line.shape[1] // SIDE

    def block(offset):
        return line[:, offset * width : (offset + 1) * width]

    return _ring_scatter(block, second, _halves)


def _reorder_kernel(by_x, by_z, inverse_ref, rows_ref, *out_refs):
    rows = rows_ref[...]
    normed = (rows.astype(jnp.float32) * inverse_ref[...][:, :1]).astype(jnp.bfloat16)
    for ref, value in zip(out_refs, (rows, rows, normed, normed)):
        ref[...] = value


def _reorder(embeddings, inverse, x, z):
    rows, features = embeddings.shape
    blocks = SIDE * SIDE
    width = features // blocks
    block = jnp.arange(blocks, dtype=jnp.int32)
    off_x = (block // SIDE - x + SIDE) % SIDE
    off_z = (block % SIDE - z + SIDE) % SIDE
    whole = (rows, width)
    along_x = pl.BlockSpec(whole, lambda i, by_x, by_z: (0, by_x[i]))
    along_z = pl.BlockSpec(whole, lambda i, by_x, by_z: (0, by_z[i]))
    shape = jax.ShapeDtypeStruct(embeddings.shape, jnp.bfloat16)
    return pl.pallas_call(
        _reorder_kernel,
        grid_spec=pltpu.PrefetchScalarGridSpec(
            num_scalar_prefetch=2,
            grid=(blocks,),
            in_specs=[
                pl.BlockSpec((rows, 128), lambda i, by_x, by_z: (0, 0)),
                pl.BlockSpec(whole, lambda i, by_x, by_z: (0, i)),
            ],
            out_specs=[along_x, along_z, along_x, along_z],
        ),
        out_shape=[shape] * 4,
        cost_estimate=pl.CostEstimate(
            flops=rows * features, bytes_accessed=10 * rows * features, transcendentals=0
        ),
        compiler_params=pltpu.CompilerParams(vmem_limit_bytes=32 * 1024 * 1024),
    )(off_x * SIDE + off_z, off_z * SIDE + off_x, inverse, embeddings)


def on_device(embeddings, centroids):
    row_count = embeddings.shape[0]
    local_k = centroids.shape[0]
    half = local_k // 2
    wide = embeddings.shape[1] // SIDE
    me = lax.axis_index("dp")
    x, z = me // SIDE, me % SIDE
    rows_float = embeddings.astype(jnp.float32)
    inverse = lax.rsqrt(jnp.sum(rows_float * rows_float, 1, keepdims=True) + 1e-06)
    inverse = jnp.broadcast_to(inverse, (row_count, 128))
    panel_a = _ring_panel(_z, centroids[:half])
    panel_b = _ring_panel(_x, centroids[half:])
    inverse, panel_a, panel_b = lax.optimization_barrier((inverse, panel_a, panel_b))
    rows_x, rows_z, normed_x, normed_z = (
        [array[:, i * wide : (i + 1) * wide] for i in range(SIDE)]
        for array in _reorder(embeddings, inverse, x, z)
    )
    score_a, square_a = _gather_scores(_x, panel_a, normed_x)
    score_b, square_b = _gather_scores(_z, panel_b, normed_z)
    scores = jnp.concatenate([score_a, score_b], 1)
    scale = lax.rsqrt(jnp.concatenate([square_a, square_b]) + 1e-06)
    weights = jnp.exp(scores * scale[None, :] * 20.0)
    target = row_count * lax.axis_size("dp") / (local_k * lax.axis_size("cent"))
    column = _all_sum(jnp.sum(weights, 0), "dp")
    for sweep in range(ROUNDS):
        column_scale = target / column
        row_sum = _all_sum(jnp.sum(weights * column_scale[None, :], 1), "cent")
        row_scale = 1.0 / row_sum
        if sweep + 1 < ROUNDS:
            column = _all_sum(jnp.sum(weights * row_scale[:, None], 0), "dp")
    shares = (weights * column_scale[None, :] * row_scale[:, None]).astype(jnp.bfloat16)
    mass = _all_sum(jnp.sum(shares.astype(jnp.float32), 0), "dp")
    packed = shares * PACK
    sums_a = _scatter_sums(_x, _z, packed[:, :half], rows_x)
    sums_b = _scatter_sums(_z, _x, packed[:, half:], rows_z)
    sums = jnp.concatenate([sums_a, sums_b], 0)
    new_centroids = (sums / (mass * PACK)[:, None]).astype(jnp.bfloat16)
    return (shares, new_centroids)


def solution(mesh):
    in_specs = (P("dp", None), P("cent", "dp"))
    out_specs = (P("dp", "cent"), P("cent", "dp"))
    return jax.shard_map(
        on_device, mesh=mesh, in_specs=in_specs, out_specs=out_specs, check_vma=False
    )
```

```python
import functools

import jax
import jax.numpy as jnp
from jax import lax
from jax.experimental import pallas as pl
from jax.experimental.pallas import tpu as pltpu
from jax.sharding import PartitionSpec as P

ROUNDS = 3
SIDE = 4
PACK = 0.25


def _x(step):
    return [
        (x * SIDE + z, ((x + step) % SIDE) * SIDE + z) for x in range(SIDE) for z in range(SIDE)
    ]


def _z(step):
    return [
        (x * SIDE + z, x * SIDE + (z + step) % SIDE) for x in range(SIDE) for z in range(SIDE)
    ]


def _send(value, axis, step):
    return lax.ppermute(value, "dp", axis(step))


def _ring_gather(block, axis):
    before = _send(block, axis, 1)
    after = _send(block, axis, -1)
    half = block.shape[0] // 2
    far_low = _send(before[:half], axis, 1)
    far_high = _send(after[half:], axis, -1)
    return block, after, (far_low, far_high), before


def _dot_rows(rows, block):
    return lax.dot_general(
        block, rows, (((1,), (1,)), ((), ())), preferred_element_type=jnp.float32
    )


def _squares(block):
    wide = block.astype(jnp.float32)
    return jnp.sum(wide * wide, 1)


def _ring_panel(axis, block):
    before, after, far = (_send(block, axis, step) for step in (1, -1, 2))
    return jnp.concatenate([block, after, far, before], 1)


def _gather_scores(axis, panel, rows, total):
    own, after, far, before = _ring_gather(panel, axis)
    total = total + _dot_rows(rows[1], after) + _dot_rows(rows[3], before)
    squares = _squares(own) + _squares(after) + _squares(before)
    far = jnp.concatenate(far, 0)
    return total + _dot_rows(rows[2], far), squares + _squares(far)


def _pack(value):
    return (value * PACK).astype(jnp.float16)


def _unpack(value):
    return value.astype(jnp.float32) * (1.0 / PACK)


def _ring_far(part, axis):
    low, high = part
    return _send(_pack(low), axis, 1), _send(_pack(high), axis, -1)


def _ring_near(after, before, far, axis):
    low, high = far
    rows = after.shape[0] // 2
    after = _pack(after + jnp.pad(_unpack(low), ((0, rows), (0, 0))))
    before = _pack(before + jnp.pad(_unpack(high), ((rows, 0), (0, 0))))
    return _send(after, axis, 1), _send(before, axis, -1)


CHUNK = 128
FULL = lax.Precision.HIGHEST


def _column_chunk(row, start):
    return jnp.broadcast_to(row[:, start : start + CHUNK], (CHUNK, CHUNK)).T


def _wide(column, count):
    return jnp.concatenate([column] * (count // CHUNK), 1)


def _fold(value):
    return sum(value[:, i : i + CHUNK] for i in range(0, value.shape[1], CHUNK))


def _lane_sums(folded, copies):
    ones = jnp.ones((copies, CHUNK), jnp.float32)
    return lax.dot_general(
        ones, folded, (((1,), (1,)), ((), ())), precision=FULL, preferred_element_type=jnp.float32
    )


def _row_sums_kernel(target, weights_ref, column_ref, out_ref):
    scale = target / jnp.sum(column_ref[...], 0)
    count, rows = weights_ref.shape
    total = jnp.zeros((8, rows), jnp.float32)
    for start in range(0, count, CHUNK):
        chunk = weights_ref[start : start + CHUNK, :] * _wide(_column_chunk(scale, start), rows)
        total = total + jnp.sum(chunk.reshape(CHUNK // 8, 8, rows), 0)
    total = jnp.sum(total, 0, keepdims=True)
    out_ref[...] = jnp.broadcast_to(total[None], out_ref.shape)


def _column_sums_kernel(weights_ref, row_ref, out_ref):
    scale = 1.0 / jnp.sum(row_ref[...], 0)
    count, rows = weights_ref.shape
    for start in range(0, count, CHUNK):
        folded = _fold(weights_ref[start : start + CHUNK, :] * scale)
        sums = _lane_sums(folded, out_ref.shape[0])
        out_ref[:, 0, start : start + CHUNK] = sums


def _shares_kernel(target, weights_ref, column_ref, row_ref, shares_ref, mass_ref):
    column_scale = target / jnp.sum(column_ref[...], 0)
    row_scale = 1.0 / jnp.sum(row_ref[...], 0)
    count, rows = weights_ref.shape
    for start in range(0, count, CHUNK):
        cut = slice(start, start + CHUNK)
        chunk = weights_ref[cut, :] * _wide(_column_chunk(column_scale, start), rows) * row_scale
        shares = chunk.astype(jnp.bfloat16)
        shares_ref[cut, :] = shares
        folded = _fold(shares.astype(jnp.float32))
        mass_ref[:, 0, cut] = _lane_sums(folded, mass_ref.shape[0])


def _whole(kernel, out_shape, *operands):
    inside = pl.BlockSpec(memory_space=pltpu.VMEM)
    return pl.pallas_call(
        kernel,
        out_shape=out_shape,
        in_specs=[inside] * len(operands),
        out_specs=jax.tree.map(lambda _: inside, out_shape),
        compiler_params=pltpu.CompilerParams(vmem_limit_bytes=24 * 1024 * 1024),
    )(*operands)


def _copies(axis, count):
    return jax.ShapeDtypeStruct((lax.axis_size(axis), 1, count), jnp.float32)


def _exchange(copies, axis):
    return lax.all_to_all(copies, axis, 0, 0)


def _part_kernel(slots_ref, shares_ref, rows_ref, part_ref):
    part_ref[0] = jnp.dot(shares_ref[...], rows_ref[0], preferred_element_type=jnp.float32)


def _part(shares, half, blocks, slots):
    count, rows = shares.shape[0] // 2, shares.shape[1]
    width = blocks.shape[2]
    return pl.pallas_call(
        _part_kernel,
        grid_spec=pltpu.PrefetchScalarGridSpec(
            num_scalar_prefetch=1,
            grid=slots.shape,
            in_specs=[
                pl.BlockSpec((count, rows), lambda i, slots: (half, 0)),
                pl.BlockSpec((1, rows, width), lambda i, slots: (slots[i], 0, 0)),
            ],
            out_specs=pl.BlockSpec((1, count, width), lambda i, slots: (i, 0, 0)),
        ),
        out_shape=jax.ShapeDtypeStruct((slots.size, count, width), jnp.float32),
        cost_estimate=pl.CostEstimate(flops=1000, bytes_accessed=1000, transcendentals=0),
        compiler_params=pltpu.CompilerParams(vmem_limit_bytes=12 * 1024 * 1024),
    )(slots, shares, blocks)


def _ring_far(part, axis):
    low, high = part
    return _send(low, axis, 1), _send(high, axis, -1)


def _ring_near(after, before, far, axis):
    low, high = far
    spare = after.shape[0] // 2
    after = _pack(after + jnp.pad(_unpack(low), ((0, spare), (0, 0), (0, 0))))
    before = _pack(before + jnp.pad(_unpack(high), ((spare, 0), (0, 0), (0, 0))))
    return _send(after, axis, 1), _send(before, axis, -1)


def _scatter_sums(shares, axes, blocks, slots):
    far, packed = [], []
    for half, (first, _) in enumerate(axes):
        part = _part(shares, half, blocks, slots[half][0])
        parts = _pack(part[: SIDE // 2]), _pack(part[SIDE // 2 :])
        packed.append(parts)
        far.append(_ring_far(parts, first))
    shares, packed = lax.optimization_barrier((shares, packed))
    out = []
    for half, (first, second) in enumerate(axes):
        parts = _part(shares, half, blocks, slots[half][1])
        after, before, own = (parts[i * SIDE : (i + 1) * SIDE] for i in range(SIDE - 1))
        near = _ring_near(after, before, far[half], first)
        line = [own[i] + _unpack(near[0][i]) + _unpack(near[1][i]) for i in range(SIDE)]
        came = [_send(_pack(line[i]), second, i) for i in (1, 3, 2)]
        out.append(line[0] + _unpack(came[0]) + _unpack(came[1]) + _unpack(came[2]))
    return out


def _place(place_ref, value, by_x_ref, by_z_ref):
    width = value.shape[1] // (SIDE * SIDE)
    for owner in range(SIDE * SIDE):
        off_x = lax.rem(owner // SIDE + SIDE - place_ref[0], SIDE)
        off_z = lax.rem(owner % SIDE + SIDE - place_ref[1], SIDE)
        block = value[:, owner * width : (owner + 1) * width]
        for ref, slot in ((by_x_ref, off_x * SIDE + off_z), (by_z_ref, off_z * SIDE + off_x)):
            ref[:, pl.ds(pl.multiple_of(slot * width, width), width)] = block


def _reorder_kernel(place_ref, rows_ref, by_x_ref, by_z_ref, blocks_ref):
    rows = rows_ref[...]
    width = blocks_ref.shape[2]
    for i in range(SIDE * SIDE):
        blocks_ref[i] = rows[:, i * width : (i + 1) * width]
    rows = rows.astype(jnp.float32)
    inverse = lax.rsqrt(jnp.sum(rows * rows, 1, keepdims=True) + 1e-06)
    _place(place_ref, (rows * inverse).astype(jnp.bfloat16), by_x_ref, by_z_ref)


def _reorder(embeddings, place):
    rows, features = embeddings.shape
    tile = 128
    blocks = SIDE * SIDE
    width = features // blocks
    spec = pl.BlockSpec((tile, features), lambda i, place: (i, 0))
    shape = jax.ShapeDtypeStruct(embeddings.shape, jnp.bfloat16)
    by_x, by_z, split = pl.pallas_call(
        _reorder_kernel,
        grid_spec=pltpu.PrefetchScalarGridSpec(
            num_scalar_prefetch=1,
            grid=(rows // tile,),
            in_specs=[spec],
            out_specs=[
                spec,
                spec,
                pl.BlockSpec((blocks, tile, width), lambda i, place: (0, i, 0)),
            ],
        ),
        out_shape=[shape, shape, jax.ShapeDtypeStruct((blocks, rows, width), jnp.bfloat16)],
        cost_estimate=pl.CostEstimate(
            flops=3 * rows * features, bytes_accessed=8 * rows * features, transcendentals=rows
        ),
        compiler_params=pltpu.CompilerParams(vmem_limit_bytes=24 * 1024 * 1024),
    )(place, embeddings)
    wide = features // SIDE
    by_x, by_z = (
        [part[:, i * wide : (i + 1) * wide] for i in range(SIDE)] for part in (by_x, by_z)
    )
    return by_x, by_z, split


def on_device(embeddings, centroids):
    row_count = embeddings.shape[0]
    local_k = centroids.shape[0]
    half = local_k // 2
    me = lax.axis_index("dp")
    x, z = me // SIDE, me % SIDE
    offset = jnp.arange(SIDE, dtype=jnp.int32)
    along_x, along_z = lax.rem(x + offset, SIDE), lax.rem(z + offset, SIDE)
    grid = along_x[:, None] * SIDE + along_z[None, :]
    slots = [
        (table[2], jnp.concatenate([table[1], table[3], table[0]])) for table in (grid, grid.T)
    ]
    place = jnp.stack([x, z]).astype(jnp.int32)
    panel_a = _ring_panel(_z, centroids[:half])
    panel_b = _ring_panel(_x, centroids[half:])
    place, slots, panel_a, panel_b = lax.optimization_barrier((place, slots, panel_a, panel_b))
    normed_x, normed_z, blocks = _reorder(embeddings, place)
    own_a = _dot_rows(normed_x[0], panel_a)
    own_b = _dot_rows(normed_z[0], panel_b)
    score_a, square_a = _gather_scores(_x, panel_a, normed_x, own_a)
    score_b, square_b = _gather_scores(_z, panel_b, normed_z, own_b)
    scores = jnp.concatenate([score_a, score_b], 0)
    scale = lax.rsqrt(jnp.concatenate([square_a, square_b]) + 1e-06)
    weights = jnp.exp(scores * scale[:, None] * 20.0)
    target = row_count * lax.axis_size("dp") / (local_k * lax.axis_size("cent"))
    column = jnp.broadcast_to(jnp.sum(weights, 1)[None, None], _copies("dp", local_k).shape)
    for sweep in range(ROUNDS):
        column = _exchange(column, "dp")
        row = _whole(
            functools.partial(_row_sums_kernel, target),
            _copies("cent", row_count),
            weights,
            column,
        )
        row = _exchange(row, "cent")
        if sweep + 1 < ROUNDS:
            column = _whole(_column_sums_kernel, _copies("dp", local_k), weights, row)
    shares, mass = _whole(
        functools.partial(_shares_kernel, target),
        (jax.ShapeDtypeStruct((local_k, row_count), jnp.bfloat16), _copies("dp", local_k)),
        weights,
        column,
        row,
    )
    mass = jnp.sum(_exchange(mass, "dp"), (0, 1))
    sums = _scatter_sums(
        shares, [(_x, _z), (_z, _x)], blocks, slots
    )
    sums = jnp.concatenate(sums, 0)
    new_centroids = (sums / mass[:, None]).astype(jnp.bfloat16)
    return (shares.T, new_centroids)


def solution(mesh):
    in_specs = (P("dp", None), P("cent", "dp"))
    out_specs = (P("dp", "cent"), P("cent", "dp"))
    return jax.shard_map(
        on_device, mesh=mesh, in_specs=in_specs, out_specs=out_specs, check_vma=False
    )
```

```python
import functools

import jax
import jax.numpy as jnp
from jax import lax
from jax.experimental import pallas as pl
from jax.experimental.pallas import tpu as pltpu
from jax.sharding import PartitionSpec as P

ROUNDS = 3
SIDE = 4
PACK = 0.25
MASS_ROWS = 16


def _x(step):
    return [
        (x * SIDE + z, ((x + step) % SIDE) * SIDE + z) for x in range(SIDE) for z in range(SIDE)
    ]


def _z(step):
    return [
        (x * SIDE + z, x * SIDE + (z + step) % SIDE) for x in range(SIDE) for z in range(SIDE)
    ]


def _send(value, axis, step):
    return lax.ppermute(value, "dp", axis(step))


def _dot_rows(rows, block):
    return lax.dot_general(
        block, rows, (((1,), (1,)), ((), ())), preferred_element_type=jnp.float32
    )


def _squares(block):
    wide = block.astype(jnp.float32)
    return jnp.sum(wide * wide, 1)


def _ring(block, axis):
    before, after = _send(block, axis, 1), _send(block, axis, -1)
    half = block.shape[0] // 2
    low, high = _send(before[:half], axis, 1), _send(after[half:], axis, -1)
    return after, jnp.concatenate([low, high], 0), before


def _line_panel(axis, block):
    return jnp.concatenate([block, *_ring(block, axis)], 1)


def _gather_scores(axis, panel, rows):
    after, far, before = _ring(panel, axis)
    total, squares = _dot_rows(rows[0], panel), _squares(panel)
    for own, block in ((rows[1], after), (rows[3], before)):
        total = lax.optimization_barrier(total) + _dot_rows(own, block)
        squares = squares + _squares(block)
    total = lax.optimization_barrier(total)
    return total + _dot_rows(rows[2], far), squares + _squares(far)


def _pack(value):
    return (value * PACK).astype(jnp.float16)


def _unpack(value):
    return value.astype(jnp.float32) * (1.0 / PACK)


CHUNK = 128
FULL = lax.Precision.HIGHEST


def _column_chunk(row, start):
    return jnp.broadcast_to(row[:, start : start + CHUNK], (CHUNK, CHUNK)).T


def _wide(column, count):
    return jnp.concatenate([column] * (count // CHUNK), 1)


def _fold(value):
    return sum(value[:, i : i + CHUNK] for i in range(0, value.shape[1], CHUNK))


def _lane_sums(folded, copies):
    ones = jnp.ones((copies, CHUNK), jnp.float32)
    return lax.dot_general(
        ones, folded, (((1,), (1,)), ((), ())), precision=FULL, preferred_element_type=jnp.float32
    )


def _row_sums_kernel(target, weights_ref, column_ref, out_ref):
    scale = target / jnp.sum(column_ref[...], 0)
    count, rows = weights_ref.shape
    total = jnp.zeros((8, rows), jnp.float32)
    for start in range(0, count, CHUNK):
        chunk = weights_ref[start : start + CHUNK, :] * _wide(_column_chunk(scale, start), rows)
        total = total + jnp.sum(chunk.reshape(CHUNK // 8, 8, rows), 0)
    total = jnp.sum(total, 0, keepdims=True)
    out_ref[...] = jnp.broadcast_to(total[None], out_ref.shape)


def _column_sums_kernel(weights_ref, row_ref, out_ref):
    scale = 1.0 / jnp.sum(row_ref[...], 0)
    count, rows = weights_ref.shape
    for start in range(0, count, CHUNK):
        folded = _fold(weights_ref[start : start + CHUNK, :] * scale)
        sums = _lane_sums(folded, out_ref.shape[0])
        out_ref[:, 0, start : start + CHUNK] = sums


def _shares_kernel(target, weights_ref, column_ref, row_ref, shares_ref, mass_ref):
    column_scale = target / jnp.sum(column_ref[...], 0)
    row_scale = 1.0 / jnp.sum(row_ref[...], 0)
    count, rows = weights_ref.shape
    mass_ref[...] = jnp.zeros_like(mass_ref)
    for start in range(0, count, CHUNK):
        cut = slice(start, start + CHUNK)
        chunk = weights_ref[cut, :] * _wide(_column_chunk(column_scale, start), rows) * row_scale
        shares = chunk.astype(jnp.bfloat16)
        shares_ref[cut, :] = shares
        sums = _lane_sums(_fold(shares.astype(jnp.float32)), 8)
        half, place = divmod(start, count // 2)
        row, lane = divmod(place, mass_ref.shape[2])
        mass_ref[half, row, lane : lane + CHUNK] = sums[0]


def _whole(kernel, out_shape, *operands):
    inside = pl.BlockSpec(memory_space=pltpu.VMEM)
    return pl.pallas_call(
        kernel,
        out_shape=out_shape,
        in_specs=[inside] * len(operands),
        out_specs=jax.tree.map(lambda _: inside, out_shape),
        compiler_params=pltpu.CompilerParams(vmem_limit_bytes=12 * 1024 * 1024),
    )(*operands)


def _copies(axis, count):
    return jax.ShapeDtypeStruct((lax.axis_size(axis), 1, count), jnp.float32)


def _exchange(copies, axis):
    return lax.all_to_all(copies, axis, 0, 0)


def _part_kernel(slots_ref, shares_ref, mass_ref, rows_ref, part_ref):
    count = shares_ref.shape[0]
    part_ref[0, :count] = jnp.dot(shares_ref[...], rows_ref[0], preferred_element_type=jnp.float32)
    part_ref[0, count:] = mass_ref[0]


def _part(shares, mass, half, blocks, slots, flops=1000):
    count, rows = shares.shape[0] // 2, shares.shape[1]
    width = blocks.shape[2]
    extra = mass.shape[1]
    return pl.pallas_call(
        _part_kernel,
        grid_spec=pltpu.PrefetchScalarGridSpec(
            num_scalar_prefetch=1,
            grid=slots.shape,
            in_specs=[
                pl.BlockSpec((count, rows), lambda i, slots: (half, 0)),
                pl.BlockSpec((1, extra, width), lambda i, slots: (half, 0, 0)),
                pl.BlockSpec((1, rows, width), lambda i, slots: (slots[i], 0, 0)),
            ],
            out_specs=pl.BlockSpec((1, count + extra, width), lambda i, slots: (i, 0, 0)),
        ),
        out_shape=jax.ShapeDtypeStruct((slots.size, count + extra, width), jnp.float32),
        cost_estimate=pl.CostEstimate(flops=flops, bytes_accessed=flops // 512, transcendentals=0),
        compiler_params=pltpu.CompilerParams(vmem_limit_bytes=8 * 1024 * 1024),
    )(slots, shares, mass, blocks)


def _ring_far(part, axis):
    low, high = part
    return _send(low, axis, 1), _send(high, axis, -1)


def _ring_near(after, before, far, axis):
    low, high = far
    spare = after.shape[0] // 2
    after = _pack(after + jnp.pad(_unpack(low), ((0, spare), (0, 0), (0, 0))))
    before = _pack(before + jnp.pad(_unpack(high), ((spare, 0), (0, 0), (0, 0))))
    return _send(after, axis, 1), _send(before, axis, -1)


def _scatter_sums(shares, mass, axes, blocks, slots):
    far, packed = [], []
    for half, (first, _) in enumerate(axes):
        work = 2 * shares.shape[0] * shares.shape[1] * blocks.shape[2] * SIDE
        part = _part(shares, mass, half, blocks, slots[half][0], work)
        parts = _pack(part[: SIDE // 2]), _pack(part[SIDE // 2 :])
        packed.append(parts)
        far.append(_ring_far(parts, first))
    shares, packed = lax.optimization_barrier((shares, packed))
    out = []
    for half, (first, second) in enumerate(axes):
        parts = _part(shares, mass, half, blocks, slots[half][1])
        near = _ring_near(parts[:SIDE], parts[SIDE:], far[half], first)
        own = _part(shares, mass, half, blocks, slots[half][2])
        line = [own[i] + _unpack(near[0][i]) + _unpack(near[1][i]) for i in range(SIDE)]
        came = [_send(_pack(line[i]), second, i) for i in (1, 3, 2)]
        out.append(line[0] + _unpack(came[0]) + _unpack(came[1]) + _unpack(came[2]))
    return out


def _place(place_ref, value, by_x_ref, by_z_ref):
    width = value.shape[1] // (SIDE * SIDE)
    for owner in range(SIDE * SIDE):
        off_x = lax.rem(owner // SIDE + SIDE - place_ref[0], SIDE)
        off_z = lax.rem(owner % SIDE + SIDE - place_ref[1], SIDE)
        block = value[:, owner * width : (owner + 1) * width]
        slot_x, slot_z = off_x * SIDE + off_z, off_z * SIDE + off_x
        for ref, slot in ((by_x_ref, slot_x), (by_z_ref, slot_z)):
            ref[:, pl.ds(pl.multiple_of(slot * width, width), width)] = block


def _reorder_kernel(place_ref, rows_ref, by_x_ref, by_z_ref, blocks_ref):
    rows = rows_ref[...]
    width = blocks_ref.shape[2]
    for i in range(SIDE * SIDE):
        blocks_ref[i] = rows[:, i * width : (i + 1) * width]
    rows = rows.astype(jnp.float32)
    inverse = lax.rsqrt(jnp.sum(rows * rows, 1, keepdims=True) + 1e-06)
    _place(place_ref, (rows * inverse).astype(jnp.bfloat16), by_x_ref, by_z_ref)


def _reorder(embeddings, place):
    rows, features = embeddings.shape
    tile = 128
    blocks = SIDE * SIDE
    width = features // blocks
    spec = pl.BlockSpec((tile, features), lambda i, place: (i, 0))
    shape = jax.ShapeDtypeStruct(embeddings.shape, jnp.bfloat16)
    by_x, by_z, split = pl.pallas_call(
        _reorder_kernel,
        grid_spec=pltpu.PrefetchScalarGridSpec(
            num_scalar_prefetch=1,
            grid=(rows // tile,),
            in_specs=[spec],
            out_specs=[
                spec,
                spec,
                pl.BlockSpec((blocks, tile, width), lambda i, place: (0, i, 0)),
            ],
        ),
        out_shape=[shape, shape, jax.ShapeDtypeStruct((blocks, rows, width), jnp.bfloat16)],
        cost_estimate=pl.CostEstimate(
            flops=3 * rows * features, bytes_accessed=8 * rows * features, transcendentals=rows
        ),
        compiler_params=pltpu.CompilerParams(vmem_limit_bytes=16 * 1024 * 1024),
    )(place, embeddings)
    wide = features // SIDE
    by_x, by_z = (
        [part[:, i * wide : (i + 1) * wide] for i in range(SIDE)] for part in (by_x, by_z)
    )
    return by_x, by_z, split


def on_device(embeddings, centroids):
    row_count = embeddings.shape[0]
    local_k = centroids.shape[0]
    half = local_k // 2
    me = lax.axis_index("dp")
    x, z = me // SIDE, me % SIDE
    offset = jnp.arange(SIDE, dtype=jnp.int32)
    along_x, along_z = lax.rem(x + offset, SIDE), lax.rem(z + offset, SIDE)
    grid = along_x[:, None] * SIDE + along_z[None, :]
    slots = [
        (table[2], jnp.concatenate([table[1], table[3]]), table[0]) for table in (grid, grid.T)
    ]
    place = jnp.stack([x, z]).astype(jnp.int32)
    panel_a = _line_panel(_z, centroids[:half])
    panel_b = _line_panel(_x, centroids[half:])
    place, slots, panel_a, panel_b = lax.optimization_barrier((place, slots, panel_a, panel_b))
    normed_x, normed_z, blocks = _reorder(embeddings, place)
    score_a, square_a = _gather_scores(_x, panel_a, normed_x)
    score_b, square_b = _gather_scores(_z, panel_b, normed_z)
    scores = jnp.concatenate([score_a, score_b], 0)
    scale = lax.rsqrt(jnp.concatenate([square_a, square_b]) + 1e-06)
    weights = jnp.exp(scores * scale[:, None] * 20.0)
    target = row_count * lax.axis_size("dp") / (local_k * lax.axis_size("cent"))
    column = jnp.broadcast_to(jnp.sum(weights, 1)[None, None], _copies("dp", local_k).shape)
    for sweep in range(ROUNDS):
        column = _exchange(column, "dp")
        row = _whole(
            functools.partial(_row_sums_kernel, target),
            _copies("cent", row_count),
            weights,
            column,
        )
        row = _exchange(row, "cent")
        if sweep + 1 < ROUNDS:
            column = _whole(_column_sums_kernel, _copies("dp", local_k), weights, row)
    width = centroids.shape[1]
    shares, mass = _whole(
        functools.partial(_shares_kernel, target),
        (
            jax.ShapeDtypeStruct((local_k, row_count), jnp.bfloat16),
            jax.ShapeDtypeStruct((2, MASS_ROWS, width), jnp.float32),
        ),
        weights,
        column,
        row,
    )
    sums = _scatter_sums(shares, mass, [(_x, _z), (_z, _x)], blocks, slots)
    means = []
    for total in sums:
        mass = total[half:].reshape(-1)[:half]
        means.append((total[:half] / mass[:, None]).astype(jnp.bfloat16))
    first = lax.optimization_barrier(jnp.pad(means[0], ((0, half), (0, 0))))
    return (shares.T, lax.dynamic_update_slice(first, means[1], (half, 0)))


def solution(mesh):
    in_specs = (P("dp", None), P("cent", "dp"))
    out_specs = (P("dp", "cent"), P("cent", "dp"))
    return jax.shard_map(
        on_device, mesh=mesh, in_specs=in_specs, out_specs=out_specs, check_vma=False
    )
```

```python
import functools

import jax
import jax.numpy as jnp
from jax import lax
from jax.experimental import pallas as pl
from jax.experimental.pallas import tpu as pltpu
from jax.sharding import PartitionSpec as P

ROUNDS = 3
SIDE = 4
PACK = 0.25
MASS_ROWS = 16


def _x(step):
    return [
        (x * SIDE + z, ((x + step) % SIDE) * SIDE + z) for x in range(SIDE) for z in range(SIDE)
    ]


def _z(step):
    return [
        (x * SIDE + z, x * SIDE + (z + step) % SIDE) for x in range(SIDE) for z in range(SIDE)
    ]


def _send(value, axis, step):
    return lax.ppermute(value, "dp", axis(step))


def _dot_rows(rows, block):
    return lax.dot_general(
        block, rows, (((1,), (1,)), ((), ())), preferred_element_type=jnp.float32
    )


def _squares(block):
    wide = block.astype(jnp.float32)
    return jnp.sum(wide * wide, 1)


def _ring(block, axis):
    before, after = _send(block, axis, 1), _send(block, axis, -1)
    half = block.shape[0] // 2
    low, high = _send(before[:half], axis, 1), _send(after[half:], axis, -1)
    return after, jnp.concatenate([low, high], 0), before


def _line_panel(axis, block):
    return jnp.concatenate([block, *_ring(block, axis)], 1)


def _near_scores_kernel(total_ref, after_ref, before_ref, rows_1_ref, rows_3_ref, out_ref):
    out_ref[...] = (
        total_ref[...]
        + _dot_rows(rows_1_ref[...], after_ref[...])
        + _dot_rows(rows_3_ref[...], before_ref[...])
    )


def _near_scores(total, after, before, rows):
    count, wide = after.shape
    tile = rows.shape[0] // SIDE
    panel = pl.BlockSpec((count, wide), lambda i: (0, 0))
    tiles = pl.BlockSpec((count, tile), lambda i: (0, i))
    return pl.pallas_call(
        _near_scores_kernel,
        grid=(SIDE,),
        in_specs=[
            tiles,
            panel,
            panel,
            pl.BlockSpec((tile, wide), lambda i: (i, 1)),
            pl.BlockSpec((tile, wide), lambda i: (i, 3)),
        ],
        out_specs=tiles,
        out_shape=jax.ShapeDtypeStruct(total.shape, jnp.float32),
        cost_estimate=pl.CostEstimate(
            flops=4 * count * wide * rows.shape[0],
            bytes_accessed=4 * wide * (count + rows.shape[0]) + 8 * total.size,
            transcendentals=0,
        ),
        compiler_params=pltpu.CompilerParams(vmem_limit_bytes=14 * 1024 * 1024),
    )(total, after, before, rows, rows)


def _gather_scores(axis, panel, rows):
    after, far, before = _ring(panel, axis)
    wide = panel.shape[1]
    total = _dot_rows(rows[:, :wide], panel)
    total = _near_scores(total, after, before, rows)
    squares = _squares(panel) + _squares(after) + _squares(before) + _squares(far)
    return total + _dot_rows(rows[:, 2 * wide : 3 * wide], far), squares


def _pack(value):
    return (value * PACK).astype(jnp.float16)


def _unpack(value):
    return value.astype(jnp.float32) * (1.0 / PACK)


CHUNK = 128
FULL = lax.Precision.HIGHEST


def _chunks(count, body):
    def step(i, carry):
        body(pl.ds(pl.multiple_of(i * CHUNK, CHUNK), CHUNK))
        return carry

    lax.fori_loop(0, count // CHUNK, step, 0, unroll=True)


def _column_chunk(row_ref, cut, count):
    column = jnp.broadcast_to(row_ref[:, cut], (CHUNK, CHUNK)).T
    return jnp.concatenate([column] * (count // CHUNK), 1)


def _fold(value):
    return sum(value[:, i : i + CHUNK] for i in range(0, value.shape[1], CHUNK))


def _lane_sums(folded, copies):
    ones = jnp.ones((copies, CHUNK), jnp.float32)
    return lax.dot_general(
        ones, folded, (((1,), (1,)), ((), ())), precision=FULL, preferred_element_type=jnp.float32
    )


def _row_sums_kernel(target, weights_ref, column_ref, out_ref, scale_ref, total_ref):
    scale_ref[...] = target / jnp.sum(column_ref[...], 0)
    count, rows = weights_ref.shape
    total_ref[...] = jnp.zeros_like(total_ref)

    def body(cut):
        chunk = weights_ref[cut, :] * _column_chunk(scale_ref, cut, rows)
        total_ref[...] += jnp.sum(chunk.reshape(CHUNK // 8, 8, rows), 0)

    _chunks(count, body)
    total = jnp.sum(total_ref[...], 0, keepdims=True)
    out_ref[...] = jnp.broadcast_to(total[None], out_ref.shape)


def _column_sums_kernel(weights_ref, row_ref, out_ref, scale_ref):
    scale_ref[...] = 1.0 / jnp.sum(row_ref[...], 0)

    def body(cut):
        folded = _fold(weights_ref[cut, :] * scale_ref[...])
        out_ref[:, 0, cut] = _lane_sums(folded, out_ref.shape[0])

    _chunks(weights_ref.shape[0], body)


def _shares_kernel(
    target, weights_ref, column_ref, row_ref, shares_ref, mass_ref, column_scale_ref, row_scale_ref
):
    column_scale_ref[...] = target / jnp.sum(column_ref[...], 0)
    row_scale_ref[...] = 1.0 / jnp.sum(row_ref[...], 0)
    count, rows = weights_ref.shape

    def body(cut):
        scale = _column_chunk(column_scale_ref, cut, rows) * row_scale_ref[...]
        shares = (weights_ref[cut, :] * scale).astype(jnp.bfloat16)
        shares_ref[cut, :] = shares
        column_scale_ref[:, cut] = _lane_sums(_fold(shares.astype(jnp.float32)), 8)[:1]

    _chunks(count, body)
    mass_ref[...] = jnp.zeros_like(mass_ref)
    halves, _, width = mass_ref.shape
    for start in range(0, count, width):
        half, place = divmod(start, count // halves)
        mass_ref[half, place // width] = column_scale_ref[0, start : start + width]


def _whole(kernel, out_shape, scratch, *operands):
    inside = pl.BlockSpec(memory_space=pltpu.VMEM)
    return pl.pallas_call(
        kernel,
        out_shape=out_shape,
        in_specs=[inside] * len(operands),
        out_specs=jax.tree.map(lambda _: inside, out_shape),
        scratch_shapes=[pltpu.VMEM(shape, jnp.float32) for shape in scratch],
        compiler_params=pltpu.CompilerParams(vmem_limit_bytes=12 * 1024 * 1024),
    )(*operands)


def _copies(axis, count):
    return jax.ShapeDtypeStruct((lax.axis_size(axis), 1, count), jnp.float32)


def _exchange(copies, axis):
    return lax.all_to_all(copies, axis, 0, 0)


def _part_kernel(slots_ref, shares_ref, mass_ref, rows_ref, part_ref):
    count = shares_ref.shape[0]
    part_ref[0, :count] = jnp.dot(shares_ref[...], rows_ref[0], preferred_element_type=jnp.float32)
    part_ref[0, count:] = mass_ref[0]


def _part(shares, mass, halves, blocks, slots, flops=1000):
    count, rows = shares.shape[0] // 2, shares.shape[1]
    width = blocks.shape[2]
    extra = mass.shape[1]
    first, each = halves[0], slots[0].shape[0]
    return pl.pallas_call(
        _part_kernel,
        grid_spec=pltpu.PrefetchScalarGridSpec(
            num_scalar_prefetch=1,
            grid=(len(halves), each),
            in_specs=[
                pl.BlockSpec((count, rows), lambda h, i, slots: (first + h, 0)),
                pl.BlockSpec((1, extra, width), lambda h, i, slots: (first + h, 0, 0)),
                pl.BlockSpec((1, rows, width), lambda h, i, slots: (slots[h * each + i], 0, 0)),
            ],
            out_specs=pl.BlockSpec(
                (1, count + extra, width), lambda h, i, slots: (h * each + i, 0, 0)
            ),
        ),
        out_shape=jax.ShapeDtypeStruct((len(halves) * each, count + extra, width), jnp.float32),
        cost_estimate=pl.CostEstimate(flops=flops, bytes_accessed=flops // 512, transcendentals=0),
        compiler_params=pltpu.CompilerParams(vmem_limit_bytes=8 * 1024 * 1024),
    )(jnp.concatenate(slots), shares, mass, blocks)


def _ring_far(part, axis):
    low, high = part
    return _send(low, axis, 1), _send(high, axis, -1)


def _ring_near(after, before, far, axis):
    low, high = far
    spare = after.shape[0] // 2
    after = _pack(after + jnp.pad(_unpack(low), ((0, spare), (0, 0), (0, 0))))
    before = _pack(before + jnp.pad(_unpack(high), ((spare, 0), (0, 0), (0, 0))))
    return _send(after, axis, 1), _send(before, axis, -1)


def _scatter_sums(shares, mass, axes, blocks, slots):
    far, packed = [], []
    work = 2 * shares.shape[0] * shares.shape[1] * blocks.shape[2] * SIDE
    for half, (first, _) in enumerate(axes):
        part = _part(shares, mass, [half], blocks, [slots[half][0]], work)
        parts = _pack(part[: SIDE // 2]), _pack(part[SIDE // 2 :])
        packed.append(parts)
        far.append(_ring_far(parts, first))
    shares, packed = lax.optimization_barrier((shares, packed))
    near = [_part(shares, mass, [half], blocks, [slots[half][1]]) for half in range(2)]
    own = _part(shares, mass, [0, 1], blocks, [slot[2] for slot in slots])
    out = []
    for half, (first, second) in enumerate(axes):
        ends = _ring_near(near[half][:SIDE], near[half][SIDE:], far[half], first)
        line = [
            own[SIDE * half + i] + _unpack(ends[0][i]) + _unpack(ends[1][i]) for i in range(SIDE)
        ]
        came = [_send(_pack(line[i]), second, i) for i in (1, 3, 2)]
        out.append(line[0] + _unpack(came[0]) + _unpack(came[1]) + _unpack(came[2]))
    return out


def _place(place_ref, value, by_x_ref, by_z_ref):
    width = value.shape[1] // (SIDE * SIDE)
    for owner in range(SIDE * SIDE):
        off_x = lax.rem(owner // SIDE + SIDE - place_ref[0], SIDE)
        off_z = lax.rem(owner % SIDE + SIDE - place_ref[1], SIDE)
        block = value[:, owner * width : (owner + 1) * width]
        slot_x, slot_z = off_x * SIDE + off_z, off_z * SIDE + off_x
        for ref, slot in ((by_x_ref, slot_x), (by_z_ref, slot_z)):
            ref[:, pl.ds(pl.multiple_of(slot * width, width), width)] = block


def _reorder_kernel(place_ref, rows_ref, by_x_ref, by_z_ref, blocks_ref):
    rows = rows_ref[...]
    width = blocks_ref.shape[2]
    for i in range(SIDE * SIDE):
        blocks_ref[i] = rows[:, i * width : (i + 1) * width]
    rows = rows.astype(jnp.float32)
    inverse = lax.rsqrt(jnp.sum(rows * rows, 1, keepdims=True) + 1e-06)
    _place(place_ref, (rows * inverse).astype(jnp.bfloat16), by_x_ref, by_z_ref)


def _reorder(embeddings, place):
    rows, features = embeddings.shape
    tile = 128
    blocks = SIDE * SIDE
    width = features // blocks
    spec = pl.BlockSpec((tile, features), lambda i, place: (i, 0))
    shape = jax.ShapeDtypeStruct(embeddings.shape, jnp.bfloat16)
    by_x, by_z, split = pl.pallas_call(
        _reorder_kernel,
        grid_spec=pltpu.PrefetchScalarGridSpec(
            num_scalar_prefetch=1,
            grid=(rows // tile,),
            in_specs=[spec],
            out_specs=[
                spec,
                spec,
                pl.BlockSpec((blocks, tile, width), lambda i, place: (0, i, 0)),
            ],
        ),
        out_shape=[shape, shape, jax.ShapeDtypeStruct((blocks, rows, width), jnp.bfloat16)],
        cost_estimate=pl.CostEstimate(
            flops=3 * rows * features, bytes_accessed=8 * rows * features, transcendentals=rows
        ),
        compiler_params=pltpu.CompilerParams(vmem_limit_bytes=16 * 1024 * 1024),
    )(place, embeddings)
    return by_x, by_z, split


def on_device(embeddings, centroids):
    row_count = embeddings.shape[0]
    local_k = centroids.shape[0]
    half = local_k // 2
    me = lax.axis_index("dp")
    x, z = me // SIDE, me % SIDE
    offset = jnp.arange(SIDE, dtype=jnp.int32)
    along_x, along_z = lax.rem(x + offset, SIDE), lax.rem(z + offset, SIDE)
    grid = along_x[:, None] * SIDE + along_z[None, :]
    slots = [
        (table[2], jnp.concatenate([table[1], table[3]]), table[0]) for table in (grid, grid.T)
    ]
    place = jnp.stack([x, z]).astype(jnp.int32)
    panel_a = _line_panel(_z, centroids[:half])
    panel_b = _line_panel(_x, centroids[half:])
    place, slots, panel_a, panel_b = lax.optimization_barrier((place, slots, panel_a, panel_b))
    normed_x, normed_z, blocks = _reorder(embeddings, place)
    score_a, square_a = _gather_scores(_x, panel_a, normed_x)
    score_b, square_b = _gather_scores(_z, panel_b, normed_z)
    scores = jnp.concatenate([score_a, score_b], 0)
    scale = lax.rsqrt(jnp.concatenate([square_a, square_b]) + 1e-06)
    weights = jnp.exp(scores * scale[:, None] * 20.0)
    target = row_count * lax.axis_size("dp") / (local_k * lax.axis_size("cent"))
    column = jnp.broadcast_to(jnp.sum(weights, 1)[None, None], _copies("dp", local_k).shape)
    for sweep in range(ROUNDS):
        column = _exchange(column, "dp")
        row = _whole(
            functools.partial(_row_sums_kernel, target),
            _copies("cent", row_count),
            [(1, local_k), (8, row_count)],
            weights,
            column,
        )
        row = _exchange(row, "cent")
        if sweep + 1 < ROUNDS:
            column = _whole(
                _column_sums_kernel, _copies("dp", local_k), [(1, row_count)], weights, row
            )
    width = centroids.shape[1]
    shares, mass = _whole(
        functools.partial(_shares_kernel, target),
        (
            jax.ShapeDtypeStruct((local_k, row_count), jnp.bfloat16),
            jax.ShapeDtypeStruct((2, MASS_ROWS, width), jnp.float32),
        ),
        [(1, local_k), (1, row_count)],
        weights,
        column,
        row,
    )
    sums = _scatter_sums(shares, mass, [(_x, _z), (_z, _x)], blocks, slots)
    means = []
    for total in sums:
        mass = total[half:].reshape(-1)[:half]
        means.append((total[:half] / mass[:, None]).astype(jnp.bfloat16))
    first = lax.optimization_barrier(jnp.pad(means[0], ((0, half), (0, 0))))
    return (shares.T, lax.dynamic_update_slice(first, means[1], (half, 0)))


def solution(mesh):
    in_specs = (P("dp", None), P("cent", "dp"))
    out_specs = (P("dp", "cent"), P("cent", "dp"))
    return jax.shard_map(
        on_device, mesh=mesh, in_specs=in_specs, out_specs=out_specs, check_vma=False
    )
```

```python
import functools

import jax
import jax.numpy as jnp
from jax import lax
from jax.experimental import pallas as pl
from jax.experimental.pallas import tpu as pltpu
from jax.sharding import PartitionSpec as P

ROUNDS = 3
SIDE = 4
PACK = 0.25
MASS_ROWS = 16


def _x(step):
    return [
        (x * SIDE + z, ((x + step) % SIDE) * SIDE + z) for x in range(SIDE) for z in range(SIDE)
    ]


def _z(step):
    return [
        (x * SIDE + z, x * SIDE + (z + step) % SIDE) for x in range(SIDE) for z in range(SIDE)
    ]


def _send(value, axis, step):
    return lax.ppermute(value, "dp", axis(step))


def _dot_rows(rows, block):
    return lax.dot_general(
        block, rows, (((1,), (1,)), ((), ())), preferred_element_type=jnp.float32
    )


def _squares(block):
    wide = block.astype(jnp.float32)
    return jnp.sum(wide * wide, 1)


def _ring(block, axis):
    before, after = _send(block, axis, 1), _send(block, axis, -1)
    half = block.shape[0] // 2
    low, high = _send(before[:half], axis, 1), _send(after[half:], axis, -1)
    return after, jnp.concatenate([low, high], 0), before


def _line_panel(axis, block):
    return jnp.concatenate([block, *_ring(block, axis)], 1)


def _near_scores_kernel(total_ref, after_ref, before_ref, rows_1_ref, rows_3_ref, out_ref):
    out_ref[...] = (
        total_ref[...]
        + _dot_rows(rows_1_ref[...], after_ref[...])
        + _dot_rows(rows_3_ref[...], before_ref[...])
    )


def _near_scores(total, after, before, rows):
    count, wide = after.shape
    tile = rows.shape[0] // SIDE
    panel = pl.BlockSpec(memory_space=pltpu.VMEM)
    tiles = pl.BlockSpec((count, tile), lambda i: (0, i))
    return pl.pallas_call(
        _near_scores_kernel,
        grid=(SIDE,),
        in_specs=[
            tiles,
            panel,
            panel,
            pl.BlockSpec((tile, wide), lambda i: (i, 1)),
            pl.BlockSpec((tile, wide), lambda i: (i, 3)),
        ],
        out_specs=tiles,
        out_shape=jax.ShapeDtypeStruct(total.shape, jnp.float32),
        cost_estimate=pl.CostEstimate(
            flops=4 * count * wide * rows.shape[0],
            bytes_accessed=4 * wide * (count + rows.shape[0]) + 8 * total.size,
            transcendentals=0,
        ),
        compiler_params=pltpu.CompilerParams(vmem_limit_bytes=14 * 1024 * 1024),
    )(total, after, before, rows, rows)


def _gather_weights(axis, panel, rows):
    after, far, before = _ring(panel, axis)
    wide = panel.shape[1]
    total = _dot_rows(rows[:, :wide], panel)
    total = _near_scores(total, after, before, rows)
    squares = _squares(panel) + _squares(after) + _squares(before) + _squares(far)
    scores = total + _dot_rows(rows[:, 2 * wide : 3 * wide], far)
    weights = jnp.exp(scores * lax.rsqrt(squares + 1e-06)[:, None] * 20.0)
    return weights, jnp.sum(weights, 1)


def _pack(value):
    return (value * PACK).astype(jnp.float16)


def _unpack(value):
    return value.astype(jnp.float32) * (1.0 / PACK)


CHUNK = 128
FULL = lax.Precision.HIGHEST


def _chunks(refs):
    base = 0
    for ref in refs:
        for start in range(0, ref.shape[0], CHUNK):
            whole = slice(base + start, base + start + CHUNK)
            yield ref, slice(start, start + CHUNK), whole
        base += ref.shape[0]


def _column_chunk(row_ref, cut, count):
    column = jnp.broadcast_to(row_ref[:, cut], (CHUNK, CHUNK)).T
    return jnp.concatenate([column] * (count // CHUNK), 1)


def _fold(value):
    return sum(value[:, i : i + CHUNK] for i in range(0, value.shape[1], CHUNK))


def _lane_sums(folded, copies):
    ones = jnp.ones((copies, CHUNK), jnp.float32)
    return lax.dot_general(
        ones, folded, (((1,), (1,)), ((), ())), precision=FULL, preferred_element_type=jnp.float32
    )


def _row_sums_kernel(target, a_ref, b_ref, column_ref, out_ref, scale_ref):
    scale_ref[...] = target / jnp.sum(column_ref[...], 0)
    rows = a_ref.shape[1]
    total = jnp.zeros((8, rows), jnp.float32)
    for ref, cut, whole in _chunks((a_ref, b_ref)):
        chunk = ref[cut, :] * _column_chunk(scale_ref, whole, rows)
        total = total + jnp.sum(chunk.reshape(CHUNK // 8, 8, rows), 0)
    total = jnp.sum(total, 0, keepdims=True)
    out_ref[...] = jnp.broadcast_to(total[None], out_ref.shape)


def _column_sums_kernel(a_ref, b_ref, row_ref, out_ref):
    scale = 1.0 / jnp.sum(row_ref[...], 0)
    for ref, cut, whole in _chunks((a_ref, b_ref)):
        out_ref[:, 0, whole] = _lane_sums(_fold(ref[cut, :] * scale), out_ref.shape[0])


def _shares_kernel(target, a_ref, b_ref, column_ref, row_ref, shares_ref, mass_ref, scale_ref):
    scale_ref[...] = target / jnp.sum(column_ref[...], 0)
    row_scale = 1.0 / jnp.sum(row_ref[...], 0)
    mass_ref[...] = jnp.zeros_like(mass_ref)
    halves, _, width = mass_ref.shape
    for ref, cut, whole in _chunks((a_ref, b_ref)):
        scale = _column_chunk(scale_ref, whole, ref.shape[1]) * row_scale
        shares = (ref[cut, :] * scale).astype(jnp.bfloat16)
        shares_ref[whole, :] = shares
        mass = _lane_sums(_fold(shares.astype(jnp.float32)), 8)
        half, place = divmod(whole.start, shares_ref.shape[0] // halves)
        row, lane = divmod(place, width)
        mass_ref[half, row, lane : lane + CHUNK] = mass[0]


def _whole(kernel, out_shape, scratch, *operands):
    inside = pl.BlockSpec(memory_space=pltpu.VMEM)
    return pl.pallas_call(
        kernel,
        out_shape=out_shape,
        in_specs=[inside] * len(operands),
        out_specs=jax.tree.map(lambda _: inside, out_shape),
        scratch_shapes=[pltpu.VMEM(shape, jnp.float32) for shape in scratch],
        compiler_params=pltpu.CompilerParams(vmem_limit_bytes=12 * 1024 * 1024),
    )(*operands)


def _copies(axis, count):
    return jax.ShapeDtypeStruct((lax.axis_size(axis), 1, count), jnp.float32)


def _exchange(copies, axis):
    return lax.all_to_all(copies, axis, 0, 0)


def _part_kernel(halves, slots_ref, shares_ref, mass_ref, rows_ref, part_ref):
    count = shares_ref.shape[0] // 2
    each = part_ref.shape[0] // len(halves)
    for h, half in enumerate(halves):
        cut = slice(half * count, (half + 1) * count)

        def body(i, carry):
            i = h * each + i
            part_ref[i, :count] = jnp.dot(
                shares_ref[cut, :], rows_ref[slots_ref[i]], preferred_element_type=jnp.float32
            )
            part_ref[i, count:] = mass_ref[half]
            return carry

        lax.fori_loop(0, each, body, 0)


def _part(shares, mass, halves, blocks, slots, flops=1000):
    count = shares.shape[0] // 2 + mass.shape[1]
    inside = pl.BlockSpec(memory_space=pltpu.VMEM)
    slots = jnp.concatenate(slots)
    return pl.pallas_call(
        functools.partial(_part_kernel, halves),
        in_specs=[pl.BlockSpec(memory_space=pltpu.SMEM), inside, inside, inside],
        out_specs=inside,
        out_shape=jax.ShapeDtypeStruct((slots.size, count, blocks.shape[2]), jnp.float32),
        cost_estimate=pl.CostEstimate(flops=flops, bytes_accessed=flops // 512, transcendentals=0),
        compiler_params=pltpu.CompilerParams(vmem_limit_bytes=24 * 1024 * 1024),
    )(slots, shares, mass, blocks)


def _ring_far(part, axis):
    low, high = part
    return _send(low, axis, 1), _send(high, axis, -1)


def _ring_near(after, before, far, axis):
    low, high = far
    spare = after.shape[0] // 2
    after = _pack(after + jnp.pad(_unpack(low), ((0, spare), (0, 0), (0, 0))))
    before = _pack(before + jnp.pad(_unpack(high), ((spare, 0), (0, 0), (0, 0))))
    return _send(after, axis, 1), _send(before, axis, -1)


def _scatter_sums(shares, mass, axes, blocks, slots):
    far, packed = [], []
    work = 2 * shares.shape[0] * shares.shape[1] * blocks.shape[2] * SIDE
    for half, (first, _) in enumerate(axes):
        part = _part(shares, mass, [half], blocks, [slots[half][0]], work)
        parts = _pack(part[: SIDE // 2]), _pack(part[SIDE // 2 :])
        packed.append(parts)
        far.append(_ring_far(parts, first))
    shares, packed = lax.optimization_barrier((shares, packed))
    near = [_part(shares, mass, [half], blocks, [slots[half][1]]) for half in range(2)]
    own = _part(shares, mass, [0, 1], blocks, [slot[2] for slot in slots])
    ends = [
        _ring_near(near[half][:SIDE], near[half][SIDE:], far[half], first)
        for half, (first, _) in enumerate(axes)
    ]
    lines, came = [], []
    for half, (_, second) in enumerate(axes):
        line = _line(own, half, ends[half])
        packed = [_pack(line[i]) for i in (1, 3, 2)]
        if half == 0:
            ends[1], packed = lax.optimization_barrier((ends[1], packed))
        lines.append(line[0])
        came.append([_send(block, second, i) for i, block in zip((1, 3, 2), packed)])
    first = _means(lines[0], came[0])
    came[1], first = lax.optimization_barrier((came[1], first))
    return first, _means(lines[1], came[1])


def _line(own, half, ends):
    return [own[SIDE * half + i] + _unpack(ends[0][i]) + _unpack(ends[1][i]) for i in range(SIDE)]


def _means(own, came):
    total = own + _unpack(came[0]) + _unpack(came[1]) + _unpack(came[2])
    count = total.shape[0] - MASS_ROWS
    mass = total[count:].reshape(-1)[:count]
    return (total[:count] / mass[:, None]).astype(jnp.bfloat16)


def _place(place_ref, value, by_x_ref, by_z_ref):
    width = value.shape[1] // (SIDE * SIDE)
    for owner in range(SIDE * SIDE):
        off_x = lax.rem(owner // SIDE + SIDE - place_ref[0], SIDE)
        off_z = lax.rem(owner % SIDE + SIDE - place_ref[1], SIDE)
        block = value[:, owner * width : (owner + 1) * width]
        slot_x, slot_z = off_x * SIDE + off_z, off_z * SIDE + off_x
        for ref, slot in ((by_x_ref, slot_x), (by_z_ref, slot_z)):
            ref[:, pl.ds(pl.multiple_of(slot * width, width), width)] = block


def _reorder_kernel(place_ref, rows_ref, by_x_ref, by_z_ref, blocks_ref):
    rows = rows_ref[...]
    width = blocks_ref.shape[2]
    for i in range(SIDE * SIDE):
        blocks_ref[i] = rows[:, i * width : (i + 1) * width]
    rows = rows.astype(jnp.float32)
    inverse = lax.rsqrt(jnp.sum(rows * rows, 1, keepdims=True) + 1e-06)
    _place(place_ref, (rows * inverse).astype(jnp.bfloat16), by_x_ref, by_z_ref)


def _reorder(embeddings, place):
    rows, features = embeddings.shape
    tile = 128
    blocks = SIDE * SIDE
    width = features // blocks
    spec = pl.BlockSpec((tile, features), lambda i, place: (i, 0))
    shape = jax.ShapeDtypeStruct(embeddings.shape, jnp.bfloat16)
    by_x, by_z, split = pl.pallas_call(
        _reorder_kernel,
        grid_spec=pltpu.PrefetchScalarGridSpec(
            num_scalar_prefetch=1,
            grid=(rows // tile,),
            in_specs=[spec],
            out_specs=[
                spec,
                spec,
                pl.BlockSpec((blocks, tile, width), lambda i, place: (0, i, 0)),
            ],
        ),
        out_shape=[shape, shape, jax.ShapeDtypeStruct((blocks, rows, width), jnp.bfloat16)],
        cost_estimate=pl.CostEstimate(
            flops=3 * rows * features, bytes_accessed=8 * rows * features, transcendentals=rows
        ),
        compiler_params=pltpu.CompilerParams(vmem_limit_bytes=16 * 1024 * 1024),
    )(place, embeddings)
    return by_x, by_z, split


def on_device(embeddings, centroids):
    row_count = embeddings.shape[0]
    local_k = centroids.shape[0]
    half = local_k // 2
    me = lax.axis_index("dp")
    x, z = me // SIDE, me % SIDE
    offset = jnp.arange(SIDE, dtype=jnp.int32)
    along_x, along_z = lax.rem(x + offset, SIDE), lax.rem(z + offset, SIDE)
    grid = along_x[:, None] * SIDE + along_z[None, :]
    slots = [
        (table[2], jnp.concatenate([table[1], table[3]]), table[0]) for table in (grid, grid.T)
    ]
    place = jnp.stack([x, z]).astype(jnp.int32)
    panel_a = _line_panel(_z, centroids[:half])
    panel_b = _line_panel(_x, centroids[half:])
    place, slots, _ = lax.optimization_barrier((place, slots, (panel_a, panel_b)))
    normed_x, normed_z, blocks = _reorder(embeddings, place)
    weights_a, sums_a = _gather_weights(_x, panel_a, normed_x)
    weights_b, sums_b = _gather_weights(_z, panel_b, normed_z)
    target = row_count * lax.axis_size("dp") / (local_k * lax.axis_size("cent"))
    column = jnp.concatenate([sums_a, sums_b])
    column = jnp.broadcast_to(column[None, None], _copies("dp", local_k).shape)
    for sweep in range(ROUNDS):
        column = _exchange(column, "dp")
        row = _whole(
            functools.partial(_row_sums_kernel, target),
            _copies("cent", row_count),
            [(1, local_k)],
            weights_a,
            weights_b,
            column,
        )
        row = _exchange(row, "cent")
        if sweep + 1 < ROUNDS:
            column = _whole(
                _column_sums_kernel, _copies("dp", local_k), [], weights_a, weights_b, row
            )
    width = centroids.shape[1]
    shares, mass = _whole(
        functools.partial(_shares_kernel, target),
        (
            jax.ShapeDtypeStruct((local_k, row_count), jnp.bfloat16),
            jax.ShapeDtypeStruct((2, MASS_ROWS, width), jnp.float32),
        ),
        [(1, local_k)],
        weights_a,
        weights_b,
        column,
        row,
    )
    first, second = _scatter_sums(shares, mass, [(_x, _z), (_z, _x)], blocks, slots)
    first = jnp.pad(first, ((0, half), (0, 0)))
    return (shares.T, lax.dynamic_update_slice(first, second, (half, 0)))


def solution(mesh):
    in_specs = (P("dp", None), P("cent", "dp"))
    out_specs = (P("dp", "cent"), P("cent", "dp"))
    return jax.shard_map(
        on_device, mesh=mesh, in_specs=in_specs, out_specs=out_specs, check_vma=False
    )
```

```python
import functools

import jax
import jax.numpy as jnp
from jax import lax
from jax.experimental import pallas as pl
from jax.experimental.pallas import tpu as pltpu
from jax.sharding import PartitionSpec as P

ROUNDS = 3
SIDE = 4
PACK = 0.25
MASS_ROWS = 16


def _x(step):
    return [
        (x * SIDE + z, ((x + step) % SIDE) * SIDE + z) for x in range(SIDE) for z in range(SIDE)
    ]


def _z(step):
    return [
        (x * SIDE + z, x * SIDE + (z + step) % SIDE) for x in range(SIDE) for z in range(SIDE)
    ]


def _send(value, axis, step):
    return lax.ppermute(value, "dp", axis(step))


def _dot_rows(rows, block):
    return lax.dot_general(
        block, rows, (((1,), (1,)), ((), ())), preferred_element_type=jnp.float32
    )


def _squares(block):
    wide = block.astype(jnp.float32)
    return jnp.sum(wide * wide, 1)


def _ring(block, axis):
    before, after = _send(block, axis, 1), _send(block, axis, -1)
    half = block.shape[0] // 2
    low, high = _send(before[:half], axis, 1), _send(after[half:], axis, -1)
    return after, jnp.concatenate([low, high], 0), before


def _line_panel(axis, block):
    return jnp.concatenate([block, *_ring(block, axis)], 1)


def _near_scores_kernel(total_ref, after_ref, before_ref, rows_1_ref, rows_3_ref, out_ref):
    out_ref[...] = (
        total_ref[...]
        + _dot_rows(rows_1_ref[...], after_ref[...])
        + _dot_rows(rows_3_ref[...], before_ref[...])
    )


def _near_scores(total, after, before, rows):
    count, wide = after.shape
    tile = rows.shape[0] // SIDE
    panel = pl.BlockSpec(memory_space=pltpu.VMEM)
    tiles = pl.BlockSpec((count, tile), lambda i: (0, i))
    return pl.pallas_call(
        _near_scores_kernel,
        grid=(SIDE,),
        in_specs=[
            tiles,
            panel,
            panel,
            pl.BlockSpec((tile, wide), lambda i: (i, 1)),
            pl.BlockSpec((tile, wide), lambda i: (i, 3)),
        ],
        out_specs=tiles,
        out_shape=jax.ShapeDtypeStruct(total.shape, jnp.float32),
        cost_estimate=pl.CostEstimate(
            flops=4 * count * wide * rows.shape[0],
            bytes_accessed=4 * wide * (count + rows.shape[0]) + 8 * total.size,
            transcendentals=0,
        ),
        compiler_params=pltpu.CompilerParams(vmem_limit_bytes=14 * 1024 * 1024),
    )(total, after, before, rows, rows)


def _gather_weights(axis, panel, rows):
    after, far, before = _ring(panel, axis)
    wide = panel.shape[1]
    total = _dot_rows(rows[:, :wide], panel)
    total = _near_scores(total, after, before, rows)
    squares = _squares(panel) + _squares(after) + _squares(before) + _squares(far)
    scores = total + _dot_rows(rows[:, 2 * wide : 3 * wide], far)
    weights = jnp.exp(scores * lax.rsqrt(squares + 1e-06)[:, None] * 20.0)
    return weights, jnp.sum(weights, 1)


def _pack(value):
    return (value * PACK).astype(jnp.float16)


def _unpack(value):
    return value.astype(jnp.float32) * (1.0 / PACK)


CHUNK = 128


def _chunks(refs):
    base = 0
    for ref in refs:
        for start in range(0, ref.shape[0], CHUNK):
            whole = slice(base + start, base + start + CHUNK)
            yield ref, slice(start, start + CHUNK), whole
        base += ref.shape[0]


def _column_chunk(row_ref, cut, count):
    column = jnp.broadcast_to(row_ref[:, cut], (CHUNK, CHUNK)).T
    return jnp.concatenate([column] * (count // CHUNK), 1)


def _fold(value):
    return sum(value[:, i : i + CHUNK] for i in range(0, value.shape[1], CHUNK))


def _lane_sums(folded):
    return jnp.sum(folded.T, 0, keepdims=True)


def _row_sums_kernel(target, a_ref, b_ref, column_ref, out_ref, scale_ref):
    scale_ref[...] = target / jnp.sum(column_ref[...], 0)
    rows = a_ref.shape[1]
    total = jnp.zeros((8, rows), jnp.float32)
    for ref, cut, whole in _chunks((a_ref, b_ref)):
        chunk = ref[cut, :] * _column_chunk(scale_ref, whole, rows)
        total = total + jnp.sum(chunk.reshape(CHUNK // 8, 8, rows), 0)
    total = jnp.sum(total, 0, keepdims=True)
    out_ref[...] = jnp.broadcast_to(total[None], out_ref.shape)


def _column_sums_kernel(a_ref, b_ref, row_ref, out_ref):
    scale = 1.0 / jnp.sum(row_ref[...], 0)
    for ref, cut, whole in _chunks((a_ref, b_ref)):
        sums = _lane_sums(_fold(ref[cut, :] * scale))
        out_ref[:, 0, whole] = jnp.broadcast_to(sums, (out_ref.shape[0], CHUNK))


def _shares_kernel(target, a_ref, b_ref, column_ref, row_ref, shares_ref, mass_ref, scale_ref):
    scale_ref[...] = target / jnp.sum(column_ref[...], 0)
    row_scale = 1.0 / jnp.sum(row_ref[...], 0)
    mass_ref[...] = jnp.zeros_like(mass_ref)
    halves, _, width = mass_ref.shape
    for ref, cut, whole in _chunks((a_ref, b_ref)):
        scale = _column_chunk(scale_ref, whole, ref.shape[1]) * row_scale
        shares = (ref[cut, :] * scale).astype(jnp.bfloat16)
        shares_ref[whole, :] = shares
        mass = _lane_sums(_fold(shares.astype(jnp.float32)))
        half, place = divmod(whole.start, shares_ref.shape[0] // halves)
        row, lane = divmod(place, width)
        mass_ref[half, row, lane : lane + CHUNK] = mass[0]


def _whole(kernel, out_shape, scratch, *operands):
    inside = pl.BlockSpec(memory_space=pltpu.VMEM)
    return pl.pallas_call(
        kernel,
        out_shape=out_shape,
        in_specs=[inside] * len(operands),
        out_specs=jax.tree.map(lambda _: inside, out_shape),
        scratch_shapes=[pltpu.VMEM(shape, jnp.float32) for shape in scratch],
        compiler_params=pltpu.CompilerParams(vmem_limit_bytes=12 * 1024 * 1024),
    )(*operands)


def _copies(axis, count):
    return jax.ShapeDtypeStruct((lax.axis_size(axis), 1, count), jnp.float32)


def _exchange(copies, axis):
    return lax.all_to_all(copies, axis, 0, 0)


def _part_kernel(halves, slots_ref, shares_ref, mass_ref, rows_ref, part_ref):
    count = shares_ref.shape[0] // 2
    each = part_ref.shape[0] // len(halves)
    for h, half in enumerate(halves):
        cut = slice(half * count, (half + 1) * count)

        def body(i, carry):
            i = h * each + i
            part_ref[i, :count] = jnp.dot(
                shares_ref[cut, :], rows_ref[slots_ref[i]], preferred_element_type=jnp.float32
            )
            part_ref[i, count:] = mass_ref[half]
            return carry

        lax.fori_loop(0, each, body, 0)


def _part(shares, mass, halves, blocks, slots, flops=1000):
    count = shares.shape[0] // 2 + mass.shape[1]
    inside = pl.BlockSpec(memory_space=pltpu.VMEM)
    slots = jnp.concatenate(slots)
    return pl.pallas_call(
        functools.partial(_part_kernel, halves),
        in_specs=[pl.BlockSpec(memory_space=pltpu.SMEM), inside, inside, inside],
        out_specs=inside,
        out_shape=jax.ShapeDtypeStruct((slots.size, count, blocks.shape[2]), jnp.float32),
        cost_estimate=pl.CostEstimate(flops=flops, bytes_accessed=flops // 512, transcendentals=0),
        compiler_params=pltpu.CompilerParams(vmem_limit_bytes=24 * 1024 * 1024),
    )(slots, shares, mass, blocks)


def _ring_far(part, axis):
    low, high = part
    return _send(low, axis, 1), _send(high, axis, -1)


def _ring_near(after, before, far, axis):
    low, high = far
    spare = after.shape[0] // 2
    after = _pack(after + jnp.pad(_unpack(low), ((0, spare), (0, 0), (0, 0))))
    before = _pack(before + jnp.pad(_unpack(high), ((spare, 0), (0, 0), (0, 0))))
    return _send(after, axis, 1), _send(before, axis, -1)


def _scatter_sums(shares, mass, axes, blocks, slots):
    far, packed = [], []
    work = 2 * shares.shape[0] * shares.shape[1] * blocks.shape[2] * SIDE
    for half, (first, _) in enumerate(axes):
        part = _part(shares, mass, [half], blocks, [slots[half][0]], work)
        parts = _pack(part[: SIDE // 2]), _pack(part[SIDE // 2 :])
        packed.append(parts)
        far.append(_ring_far(parts, first))
    shares, packed = lax.optimization_barrier((shares, packed))
    near = [_part(shares, mass, [half], blocks, [slots[half][1]]) for half in range(2)]
    own = _part(shares, mass, [0, 1], blocks, [slot[2] for slot in slots])
    ends = [
        _ring_near(near[half][:SIDE], near[half][SIDE:], far[half], first)
        for half, (first, _) in enumerate(axes)
    ]
    lines, came = [], []
    for half, (_, second) in enumerate(axes):
        line = _line(own, half, ends[half])
        packed = [_pack(line[i]) for i in (1, 3, 2)]
        if half == 0:
            ends[1], packed = lax.optimization_barrier((ends[1], packed))
        lines.append(line[0])
        came.append([_send(block, second, i) for i, block in zip((1, 3, 2), packed)])
    first = _means(lines[0], came[0])
    came[1], first = lax.optimization_barrier((came[1], first))
    return first, _means(lines[1], came[1])


def _line(own, half, ends):
    return [own[SIDE * half + i] + _unpack(ends[0][i]) + _unpack(ends[1][i]) for i in range(SIDE)]


def _means(own, came):
    total = own + _unpack(came[0]) + _unpack(came[1]) + _unpack(came[2])
    count = total.shape[0] - MASS_ROWS
    mass = total[count:].reshape(-1)[:count]
    return (total[:count] / mass[:, None]).astype(jnp.bfloat16)


def _place(place_ref, value, by_x_ref, by_z_ref):
    width = value.shape[1] // (SIDE * SIDE)
    for owner in range(SIDE * SIDE):
        off_x = lax.rem(owner // SIDE + SIDE - place_ref[0], SIDE)
        off_z = lax.rem(owner % SIDE + SIDE - place_ref[1], SIDE)
        block = value[:, owner * width : (owner + 1) * width]
        slot_x, slot_z = off_x * SIDE + off_z, off_z * SIDE + off_x
        for ref, slot in ((by_x_ref, slot_x), (by_z_ref, slot_z)):
            ref[:, pl.ds(pl.multiple_of(slot * width, width), width)] = block


def _reorder_kernel(place_ref, rows_ref, by_x_ref, by_z_ref, blocks_ref):
    rows = rows_ref[...]
    width = blocks_ref.shape[2]
    for i in range(SIDE * SIDE):
        blocks_ref[i] = rows[:, i * width : (i + 1) * width]
    rows = rows.astype(jnp.float32)
    inverse = lax.rsqrt(jnp.sum(rows * rows, 1, keepdims=True) + 1e-06)
    _place(place_ref, (rows * inverse).astype(jnp.bfloat16), by_x_ref, by_z_ref)


def _reorder(embeddings, place):
    rows, features = embeddings.shape
    tile = 128
    blocks = SIDE * SIDE
    width = features // blocks
    spec = pl.BlockSpec((tile, features), lambda i, place: (i, 0))
    shape = jax.ShapeDtypeStruct(embeddings.shape, jnp.bfloat16)
    by_x, by_z, split = pl.pallas_call(
        _reorder_kernel,
        grid_spec=pltpu.PrefetchScalarGridSpec(
            num_scalar_prefetch=1,
            grid=(rows // tile,),
            in_specs=[spec],
            out_specs=[
                spec,
                spec,
                pl.BlockSpec((blocks, tile, width), lambda i, place: (0, i, 0)),
            ],
        ),
        out_shape=[shape, shape, jax.ShapeDtypeStruct((blocks, rows, width), jnp.bfloat16)],
        cost_estimate=pl.CostEstimate(
            flops=3 * rows * features, bytes_accessed=8 * rows * features, transcendentals=rows
        ),
        compiler_params=pltpu.CompilerParams(vmem_limit_bytes=16 * 1024 * 1024),
    )(place, embeddings)
    return by_x, by_z, split


def on_device(embeddings, centroids):
    row_count = embeddings.shape[0]
    local_k = centroids.shape[0]
    half = local_k // 2
    me = lax.axis_index("dp")
    x, z = me // SIDE, me % SIDE
    offset = jnp.arange(SIDE, dtype=jnp.int32)
    along_x, along_z = lax.rem(x + offset, SIDE), lax.rem(z + offset, SIDE)
    grid = along_x[:, None] * SIDE + along_z[None, :]
    slots = [
        (table[2], jnp.concatenate([table[1], table[3]]), table[0]) for table in (grid, grid.T)
    ]
    place = jnp.stack([x, z]).astype(jnp.int32)
    panel_a = _line_panel(_z, centroids[:half])
    panel_b = _line_panel(_x, centroids[half:])
    place, slots, _ = lax.optimization_barrier((place, slots, (panel_a, panel_b)))
    normed_x, normed_z, blocks = _reorder(embeddings, place)
    weights_a, sums_a = _gather_weights(_x, panel_a, normed_x)
    weights_b, sums_b = _gather_weights(_z, panel_b, normed_z)
    target = row_count * lax.axis_size("dp") / (local_k * lax.axis_size("cent"))
    column = jnp.concatenate([sums_a, sums_b])
    column = jnp.broadcast_to(column[None, None], _copies("dp", local_k).shape)
    for sweep in range(ROUNDS):
        column = _exchange(column, "dp")
        row = _whole(
            functools.partial(_row_sums_kernel, target),
            _copies("cent", row_count),
            [(1, local_k)],
            weights_a,
            weights_b,
            column,
        )
        row = _exchange(row, "cent")
        if sweep + 1 < ROUNDS:
            column = _whole(
                _column_sums_kernel, _copies("dp", local_k), [], weights_a, weights_b, row
            )
    width = centroids.shape[1]
    shares, mass = _whole(
        functools.partial(_shares_kernel, target),
        (
            jax.ShapeDtypeStruct((local_k, row_count), jnp.bfloat16),
            jax.ShapeDtypeStruct((2, MASS_ROWS, width), jnp.float32),
        ),
        [(1, local_k)],
        weights_a,
        weights_b,
        column,
        row,
    )
    first, second = _scatter_sums(shares, mass, [(_x, _z), (_z, _x)], blocks, slots)
    first = jnp.pad(first, ((0, half), (0, 0)))
    return (shares.T, lax.dynamic_update_slice(first, second, (half, 0)))


def solution(mesh):
    in_specs = (P("dp", None), P("cent", "dp"))
    out_specs = (P("dp", "cent"), P("cent", "dp"))
    return jax.shard_map(
        on_device, mesh=mesh, in_specs=in_specs, out_specs=out_specs, check_vma=False
    )
```

```python
import functools

import jax
import jax.numpy as jnp
from jax import lax
from jax.experimental import pallas as pl
from jax.experimental.pallas import tpu as pltpu
from jax.sharding import PartitionSpec as P

ROUNDS = 3
SIDE = 4
PACK = 0.25
MASS_ROWS = 16


def _x(step):
    return [
        (x * SIDE + z, ((x + step) % SIDE) * SIDE + z) for x in range(SIDE) for z in range(SIDE)
    ]


def _z(step):
    return [
        (x * SIDE + z, x * SIDE + (z + step) % SIDE) for x in range(SIDE) for z in range(SIDE)
    ]


def _send(value, axis, step):
    return lax.ppermute(value, "dp", axis(step))


def _dot_rows(rows, block):
    return lax.dot_general(
        block, rows, (((1,), (1,)), ((), ())), preferred_element_type=jnp.float32
    )


def _squares(block):
    wide = block.astype(jnp.float32)
    return jnp.sum(wide * wide, 1)


def _ring(block, axis):
    before, after = _send(block, axis, 1), _send(block, axis, -1)
    half = block.shape[0] // 2
    low, high = _send(before[:half], axis, 1), _send(after[half:], axis, -1)
    return after, jnp.concatenate([low, high], 0), before


def _line_panel(axis, block):
    return jnp.concatenate([block, *_ring(block, axis)], 1)


def _near_scores_kernel(total_ref, after_ref, before_ref, rows_1_ref, rows_3_ref, out_ref):
    out_ref[...] = (
        total_ref[...]
        + _dot_rows(rows_1_ref[...], after_ref[...])
        + _dot_rows(rows_3_ref[...], before_ref[...])
    )


def _near_scores(total, after, before, rows):
    count, wide = after.shape
    tile = rows.shape[0] // SIDE
    panel = pl.BlockSpec(memory_space=pltpu.VMEM)
    tiles = pl.BlockSpec((count, tile), lambda i: (0, i))
    return pl.pallas_call(
        _near_scores_kernel,
        grid=(SIDE,),
        in_specs=[
            tiles,
            panel,
            panel,
            pl.BlockSpec((tile, wide), lambda i: (i, 1)),
            pl.BlockSpec((tile, wide), lambda i: (i, 3)),
        ],
        out_specs=tiles,
        out_shape=jax.ShapeDtypeStruct(total.shape, jnp.float32),
        cost_estimate=pl.CostEstimate(
            flops=4 * count * wide * rows.shape[0],
            bytes_accessed=4 * wide * (count + rows.shape[0]) + 8 * total.size,
            transcendentals=0,
        ),
        compiler_params=pltpu.CompilerParams(vmem_limit_bytes=14 * 1024 * 1024),
    )(total, after, before, rows, rows)


def _gather_weights(axis, panel, rows):
    after, far, before = _ring(panel, axis)
    wide = panel.shape[1]
    total = _dot_rows(rows[:, :wide], panel)
    total = _near_scores(total, after, before, rows)
    squares = _squares(panel) + _squares(after) + _squares(before) + _squares(far)
    scores = total + _dot_rows(rows[:, 2 * wide : 3 * wide], far)
    weights = jnp.exp(scores * lax.rsqrt(squares + 1e-06)[:, None] * 20.0)
    return weights, jnp.sum(weights, 1)


def _pack(value):
    return (value * PACK).astype(jnp.float16)


def _unpack(value):
    return value.astype(jnp.float32) * (1.0 / PACK)


CHUNK = 128


def _chunks(refs):
    base = 0
    for ref in refs:
        for start in range(0, ref.shape[0], CHUNK):
            whole = slice(base + start, base + start + CHUNK)
            yield ref, slice(start, start + CHUNK), whole
        base += ref.shape[0]


def _column_chunk(row_ref, cut, count):
    column = jnp.broadcast_to(row_ref[:, cut], (CHUNK, CHUNK)).T
    return jnp.concatenate([column] * (count // CHUNK), 1)


def _fold(value):
    return sum(value[:, i : i + CHUNK] for i in range(0, value.shape[1], CHUNK))


def _lane_sums(folded):
    return jnp.sum(folded.T, 0, keepdims=True)


def _row_sums_kernel(target, a_ref, b_ref, column_ref, out_ref, scale_ref):
    scale_ref[...] = target / jnp.sum(column_ref[...], 0)
    rows = a_ref.shape[1]
    total = jnp.zeros((8, rows), jnp.float32)
    for ref, cut, whole in _chunks((a_ref, b_ref)):
        chunk = ref[cut, :] * _column_chunk(scale_ref, whole, rows)
        total = total + jnp.sum(chunk.reshape(CHUNK // 8, 8, rows), 0)
    total = jnp.sum(total, 0, keepdims=True)
    out_ref[...] = jnp.broadcast_to(total[None], out_ref.shape)


def _column_sums_kernel(a_ref, b_ref, row_ref, out_ref):
    scale = 1.0 / jnp.sum(row_ref[...], 0)
    for ref, cut, whole in _chunks((a_ref, b_ref)):
        sums = _lane_sums(_fold(ref[cut, :] * scale))
        out_ref[:, 0, whole] = jnp.broadcast_to(sums, (out_ref.shape[0], CHUNK))


def _shares_kernel(target, a_ref, b_ref, column_ref, row_ref, shares_ref, mass_ref, scale_ref):
    scale_ref[...] = target / jnp.sum(column_ref[...], 0)
    row_scale = 1.0 / jnp.sum(row_ref[...], 0)
    mass_ref[...] = jnp.zeros_like(mass_ref)
    halves, _, width = mass_ref.shape
    for ref, cut, whole in _chunks((a_ref, b_ref)):
        scale = _column_chunk(scale_ref, whole, ref.shape[1]) * row_scale
        shares = (ref[cut, :] * scale).astype(jnp.bfloat16)
        shares_ref[whole, :] = shares
        mass = _lane_sums(_fold(shares.astype(jnp.float32)))
        half, place = divmod(whole.start, shares_ref.shape[0] // halves)
        row, lane = divmod(place, width)
        mass_ref[half, row, lane : lane + CHUNK] = mass[0]


def _whole(kernel, out_shape, scratch, *operands):
    inside = pl.BlockSpec(memory_space=pltpu.VMEM)
    return pl.pallas_call(
        kernel,
        out_shape=out_shape,
        in_specs=[inside] * len(operands),
        out_specs=jax.tree.map(lambda _: inside, out_shape),
        scratch_shapes=[pltpu.VMEM(shape, jnp.float32) for shape in scratch],
        compiler_params=pltpu.CompilerParams(vmem_limit_bytes=12 * 1024 * 1024),
    )(*operands)


def _copies(axis, count):
    return jax.ShapeDtypeStruct((lax.axis_size(axis), 1, count), jnp.float32)


def _exchange(copies, axis):
    return lax.all_to_all(copies, axis, 0, 0)


def _part_kernel(halves, slots_ref, shares_ref, mass_ref, rows_ref, part_ref):
    count = shares_ref.shape[0] // 2
    each = part_ref.shape[0] // len(halves)
    for h, half in enumerate(halves):
        cut = slice(half * count, (half + 1) * count)

        def body(i, carry):
            i = h * each + i
            part_ref[i, :count] = jnp.dot(
                shares_ref[cut, :], rows_ref[slots_ref[i]], preferred_element_type=jnp.float32
            )
            part_ref[i, count:] = mass_ref[half]
            return carry

        lax.fori_loop(0, each, body, 0, unroll=each if len(halves) * each == SIDE else 1)


def _part(shares, mass, halves, blocks, slots, flops=1000):
    count = shares.shape[0] // 2 + mass.shape[1]
    inside = pl.BlockSpec(memory_space=pltpu.VMEM)
    slots = jnp.concatenate(slots)
    return pl.pallas_call(
        functools.partial(_part_kernel, halves),
        in_specs=[pl.BlockSpec(memory_space=pltpu.SMEM), inside, inside, inside],
        out_specs=inside,
        out_shape=jax.ShapeDtypeStruct((slots.size, count, blocks.shape[2]), jnp.float32),
        cost_estimate=pl.CostEstimate(flops=flops, bytes_accessed=flops // 512, transcendentals=0),
        compiler_params=pltpu.CompilerParams(vmem_limit_bytes=24 * 1024 * 1024),
    )(slots, shares, mass, blocks)


def _ring_far(part, axis):
    low, high = part
    return _send(low, axis, 1), _send(high, axis, -1)


def _ring_near(after, before, far, axis):
    low, high = far
    spare = after.shape[0] // 2
    after = _pack(after + jnp.pad(_unpack(low), ((0, spare), (0, 0), (0, 0))))
    before = _pack(before + jnp.pad(_unpack(high), ((spare, 0), (0, 0), (0, 0))))
    return _send(after, axis, 1), _send(before, axis, -1)


def _scatter_sums(shares, mass, axes, blocks, slots):
    far, packed = [], []
    work = 2 * shares.shape[0] * shares.shape[1] * blocks.shape[2] * SIDE
    for half, (first, _) in enumerate(axes):
        part = _part(shares, mass, [half], blocks, [slots[half][0]], work)
        parts = _pack(part[: SIDE // 2]), _pack(part[SIDE // 2 :])
        packed.append(parts)
        far.append(_ring_far(parts, first))
    shares, packed = lax.optimization_barrier((shares, packed))
    near = [_part(shares, mass, [half], blocks, [slots[half][1]]) for half in range(2)]
    own = _part(shares, mass, [0, 1], blocks, [slot[2] for slot in slots])
    ends = [
        _ring_near(near[half][:SIDE], near[half][SIDE:], far[half], first)
        for half, (first, _) in enumerate(axes)
    ]
    lines, came = [], []
    for half, (_, second) in enumerate(axes):
        line = _line(own, half, ends[half])
        packed = [_pack(line[i]) for i in (1, 3, 2)]
        if half == 0:
            ends[1], packed = lax.optimization_barrier((ends[1], packed))
        lines.append(line[0])
        came.append([_send(block, second, i) for i, block in zip((1, 3, 2), packed)])
    first = _means(lines[0], came[0])
    came[1], first = lax.optimization_barrier((came[1], first))
    return first, _means(lines[1], came[1])


def _line(own, half, ends):
    return [own[SIDE * half + i] + _unpack(ends[0][i]) + _unpack(ends[1][i]) for i in range(SIDE)]


def _means(own, came):
    total = own + _unpack(came[0]) + _unpack(came[1]) + _unpack(came[2])
    count = total.shape[0] - MASS_ROWS
    mass = total[count:].reshape(-1)[:count]
    return (total[:count] / mass[:, None]).astype(jnp.bfloat16)


def _place(place_ref, value, by_x_ref, by_z_ref):
    width = value.shape[1] // (SIDE * SIDE)
    for owner in range(SIDE * SIDE):
        off_x = lax.rem(owner // SIDE + SIDE - place_ref[0], SIDE)
        off_z = lax.rem(owner % SIDE + SIDE - place_ref[1], SIDE)
        block = value[:, owner * width : (owner + 1) * width]
        slot_x, slot_z = off_x * SIDE + off_z, off_z * SIDE + off_x
        for ref, slot in ((by_x_ref, slot_x), (by_z_ref, slot_z)):
            ref[:, pl.ds(pl.multiple_of(slot * width, width), width)] = block


def _reorder_kernel(place_ref, rows_ref, by_x_ref, by_z_ref, blocks_ref):
    rows = rows_ref[...]
    width = blocks_ref.shape[2]
    for i in range(SIDE * SIDE):
        blocks_ref[i] = rows[:, i * width : (i + 1) * width]
    rows = rows.astype(jnp.float32)
    inverse = lax.rsqrt(jnp.sum(rows * rows, 1, keepdims=True) + 1e-06)
    _place(place_ref, (rows * inverse).astype(jnp.bfloat16), by_x_ref, by_z_ref)


def _reorder(embeddings, place):
    rows, features = embeddings.shape
    tile = 128
    blocks = SIDE * SIDE
    width = features // blocks
    spec = pl.BlockSpec((tile, features), lambda i, place: (i, 0))
    shape = jax.ShapeDtypeStruct(embeddings.shape, jnp.bfloat16)
    by_x, by_z, split = pl.pallas_call(
        _reorder_kernel,
        grid_spec=pltpu.PrefetchScalarGridSpec(
            num_scalar_prefetch=1,
            grid=(rows // tile,),
            in_specs=[spec],
            out_specs=[
                spec,
                spec,
                pl.BlockSpec((blocks, tile, width), lambda i, place: (0, i, 0)),
            ],
        ),
        out_shape=[shape, shape, jax.ShapeDtypeStruct((blocks, rows, width), jnp.bfloat16)],
        cost_estimate=pl.CostEstimate(
            flops=3 * rows * features, bytes_accessed=8 * rows * features, transcendentals=rows
        ),
        compiler_params=pltpu.CompilerParams(vmem_limit_bytes=16 * 1024 * 1024),
    )(place, embeddings)
    return by_x, by_z, split


def on_device(embeddings, centroids):
    row_count = embeddings.shape[0]
    local_k = centroids.shape[0]
    half = local_k // 2
    me = lax.axis_index("dp")
    x, z = me // SIDE, me % SIDE
    offset = jnp.arange(SIDE, dtype=jnp.int32)
    along_x, along_z = lax.rem(x + offset, SIDE), lax.rem(z + offset, SIDE)
    grid = along_x[:, None] * SIDE + along_z[None, :]
    slots = [
        (table[2], jnp.concatenate([table[1], table[3]]), table[0]) for table in (grid, grid.T)
    ]
    place = jnp.stack([x, z]).astype(jnp.int32)
    panel_a = _line_panel(_z, centroids[:half])
    panel_b = _line_panel(_x, centroids[half:])
    place, slots, _ = lax.optimization_barrier((place, slots, (panel_a, panel_b)))
    normed_x, normed_z, blocks = _reorder(embeddings, place)
    weights_a, sums_a = _gather_weights(_x, panel_a, normed_x)
    weights_b, sums_b = _gather_weights(_z, panel_b, normed_z)
    target = row_count * lax.axis_size("dp") / (local_k * lax.axis_size("cent"))
    column = jnp.concatenate([sums_a, sums_b])
    column = jnp.broadcast_to(column[None, None], _copies("dp", local_k).shape)
    for sweep in range(ROUNDS):
        column = _exchange(column, "dp")
        row = _whole(
            functools.partial(_row_sums_kernel, target),
            _copies("cent", row_count),
            [(1, local_k)],
            weights_a,
            weights_b,
            column,
        )
        row = _exchange(row, "cent")
        if sweep + 1 < ROUNDS:
            column = _whole(
                _column_sums_kernel, _copies("dp", local_k), [], weights_a, weights_b, row
            )
    width = centroids.shape[1]
    shares, mass = _whole(
        functools.partial(_shares_kernel, target),
        (
            jax.ShapeDtypeStruct((local_k, row_count), jnp.bfloat16),
            jax.ShapeDtypeStruct((2, MASS_ROWS, width), jnp.float32),
        ),
        [(1, local_k)],
        weights_a,
        weights_b,
        column,
        row,
    )
    first, second = _scatter_sums(shares, mass, [(_x, _z), (_z, _x)], blocks, slots)
    first = jnp.pad(first, ((0, half), (0, 0)))
    return (shares.T, lax.dynamic_update_slice(first, second, (half, 0)))


def solution(mesh):
    in_specs = (P("dp", None), P("cent", "dp"))
    out_specs = (P("dp", "cent"), P("cent", "dp"))
    return jax.shard_map(
        on_device, mesh=mesh, in_specs=in_specs, out_specs=out_specs, check_vma=False
    )
```
